256 devices in a mesh: pipe: 4 (over y_hi, core), expert: 16 (over z, y_lo), dp: 4 (over x).
Axes of the slice: x: 4, y: 4 (y_hi: 2, y_lo: 2; y = y_hi * 2 + y_lo), z: 8, core: 2. Of those that a mesh axis runs over, the one named last changes fastest.
Arguments:
- x_fwd: bfloat16 [4, 2048, 3584], P('pipe', 'expert'), may hold values from -6 to 6
- ids_fwd: int32 [4, 2048, 2], P('pipe', 'expert'), may hold values from 0 to 15, all different within a row; in each aligned block of 128 rows (0 to 127, 128 to 255, ..., all dimensions but the last counted through in order) at most 24 rows name the same one
- gates_fwd: float32 [4, 2048, 2], P('pipe', 'expert'), may hold values from 0.1 to 0.6
- x_bwd: bfloat16 [4, 2048, 3584], P('pipe', 'expert'), may hold values from -6 to 6
- ids_bwd: int32 [4, 2048, 2], P('pipe', 'expert'), may hold values from 0 to 15, all different within a row; in each aligned block of 128 rows (0 to 127, 128 to 255, ..., all dimensions but the last counted through in order) at most 24 rows name the same one
- gates_bwd: float32 [4, 2048, 2], P('pipe', 'expert'), may hold values from 0.1 to 0.6
- grad_in: bfloat16 [4, 2048, 3584], P('pipe', 'expert', 'dp'), may hold values from -6 to 6
- w_gate: bfloat16 [4, 16, 3584, 2048], P('pipe', 'expert', None, 'dp'), may hold values from -0.09375 to 0.09375
- w_up: bfloat16 [4, 16, 3584, 2048], P('pipe', 'expert', None, 'dp'), may hold values from -0.09375 to 0.09375
- w_down: bfloat16 [4, 16, 2048, 3584], P('pipe', 'expert', 'dp'), may hold values from -0.125 to 0.125
Outputs:
- sent_forward: bfloat16 [4, 2048, 3584], P('pipe', 'expert', 'dp')
- sent_backward: bfloat16 [4, 2048, 3584], P('pipe', 'expert', 'dp')
The draws below stay inside these ranges and needn't reach their ends.
Inputs may be any that keep to these rules, and one draw needn't show every extreme that they name: `ids_fwd`: each row names 2 different experts. Within the rows of one index of expert at one section (aligned blocks of 128 rows) no expert is named by more than 24 rows, a bound that some block reaches. `ids_bwd`: same law as ids_fwd.
All inputs are finite; a program needn't handle non-finite values.
Results may differ from the reference program's by a relative error of at most 0.0075.
Values may be sent and summed in bfloat16 or wider, within the bound.
No kernel may reach another device: no remote copies, remote signals or barrier semaphores. Data moves between devices by JAX's collectives and lax.ppermute only.
A program may use at most 128 MiB of HBM per device.

```python
import math
import jax
import jax.numpy as jnp
import numpy as np
from jax import lax

D = 3584
HIDDEN_SIZE = 2048
TOK_DEV = 128
EXPERTS = 16
TOPK = 2
CAP = 24
TOKENS = 2048
SECTIONS = 4
N_EXPERT = 16
N_DP = 4


def shard_levels(key, shape, pieces, smallest, high):
    loudness = 1.0
    for position, shards_of in pieces:
        steps = jax.random.uniform(jax.random.fold_in(jax.random.fold_in(key, 6), position), (shards_of,), jnp.float32, smallest / len(pieces), high / len(pieces))
        loudness = loudness * jnp.repeat(jnp.exp(steps), shape[position] // shards_of).reshape((-1,) + (1,) * (len(shape) - 1 - position))
    return loudness


def routed_block(key, own, number, rows, number_of, top, most, skew):
    ranking = jax.random.permutation(key, number_of)
    crowded, common = portions_of(number_of, rows * top, most, skew, True), portions_of(number_of, rows * top, most, skew, False)
    places = jnp.arange(number_of)

    def named(lengths, rotation):
        used = int((lengths > 0).sum())
        fixed = max(1, used // 4)
        moved = fixed + (places - fixed + rotation * (used - fixed)) % max(1, number_of - fixed)
        return jnp.zeros((number_of,), jnp.int32).at[ranking[jnp.where(places < fixed, places, moved)]].set(jnp.asarray(lengths, jnp.int32))

    lengths = jnp.where(number % 4 == 0, named(crowded, number // 4), named(common, number - number // 4 - 1))
    mixed = jax.random.permutation(jax.random.fold_in(own, 3), number_of)
    source_of, taker = mixed[0:number_of // 2 * 2:2], mixed[1:number_of // 2 * 2:2]
    slack = jnp.minimum(lengths[source_of] - 1, most - lengths[taker]) // 2
    slack = jnp.where((source_of == ranking[0]) | (taker == ranking[0]) | (lengths[taker] == 0), 0, jnp.maximum(slack, 0))
    moved = jax.random.randint(jax.random.fold_in(own, 4), (number_of // 2,), 0, 1 << 20) % (slack + 1)
    lengths = lengths.at[source_of].add(-moved).at[taker].add(moved)
    labels = jnp.searchsorted(jnp.cumsum(lengths), jnp.arange(rows * top), side="right").astype(jnp.int32)
    listing = labels.reshape(top, rows).T
    listing = listing[jax.random.permutation(jax.random.fold_in(own, 1), rows)]
    rotation = jax.random.randint(jax.random.fold_in(own, 2), (rows, 1), 0, top)
    return jnp.take_along_axis(listing, (jnp.arange(top)[None, :] + rotation) % top, axis=1)


def portions_of(amount, total, reach, slope, full):
    loads = [(1 << 20) // math.isqrt(grade ** slope) + 1 for grade in range(1, amount + 1)]
    largest = reach if full else min(reach, max(-(-total // amount), total * loads[0] // sum(loads)))
    least = 1 if total - largest >= amount - 1 else 0
    given, rest = [largest] + [least] * (amount - 1), total - largest - least * (amount - 1)
    while rest > 0:
        candidates = [i for i in range(1, amount) if given[i] < largest] or [i for i in range(1, amount) if given[i] < reach]
        pool, budget = sum([loads[i] for i in candidates]), rest
        for i in candidates:
            more = min(reach - given[i], max(1, budget * loads[i] // pool), rest)
            given[i] = given[i] + more
            rest = rest - more
    return np.array(given)


def centred(rng, shape, deviation, most, split=(), kind=jnp.bfloat16):
    gain = shard_levels(rng, shape, split, -0.22, 0.18) if split else 1.0
    values = jax.random.normal(rng, shape, jnp.float32) * deviation * gain
    return jnp.minimum(jnp.maximum(values, -most), most).astype(kind)


def setup_inputs(seed: int = 0) -> dict:
    key_list = jax.random.split(jax.random.key(seed), 11)
    x_fwd = centred(key_list[0], (SECTIONS, TOKENS, D), 1.0, 6.0, ((0, 4), (1, 16)))
    ids_fwd_keys = jax.random.split(jax.random.fold_in(key_list[1], 1), SECTIONS * TOKENS // TOK_DEV)
    ids_fwd_turns = jax.random.permutation(jax.random.fold_in(key_list[1], 3), SECTIONS * TOKENS // TOK_DEV)
    ids_fwd = jax.vmap(lambda own, number: routed_block(jax.random.fold_in(key_list[1], 2), own, number, TOK_DEV, EXPERTS, TOPK, CAP, 2))(ids_fwd_keys, ids_fwd_turns).reshape((SECTIONS, TOKENS, TOPK))
    gates_fwd = jnp.clip(0.1 + 0.5 * jax.random.uniform(key_list[2], (SECTIONS, TOKENS, TOPK), jnp.float32) ** shard_levels(key_list[2], (SECTIONS, TOKENS, TOPK), ((0, 4), (1, 16)), -0.2, 0.2), 0.1, 0.6)
    x_bwd = centred(key_list[3], (SECTIONS, TOKENS, D), 1.0, 6.0, ((0, 4), (1, 16)))
    ids_bwd_keys = jax.random.split(jax.random.fold_in(key_list[4], 1), SECTIONS * TOKENS // TOK_DEV)
    ids_bwd_turns = jax.random.permutation(jax.random.fold_in(key_list[4], 3), SECTIONS * TOKENS // TOK_DEV)
    ids_bwd = jax.vmap(lambda own, number: routed_block(jax.random.fold_in(key_list[4], 2), own, number, TOK_DEV, EXPERTS, TOPK, CAP, 2))(ids_bwd_keys, ids_bwd_turns).reshape((SECTIONS, TOKENS, TOPK))
    gates_bwd = jnp.clip(0.1 + 0.5 * jax.random.uniform(key_list[5], (SECTIONS, TOKENS, TOPK), jnp.float32) ** shard_levels(key_list[5], (SECTIONS, TOKENS, TOPK), ((0, 4), (1, 16)), -0.2, 0.2), 0.1, 0.6)
    grad_in = centred(key_list[6], (SECTIONS, TOKENS, D), 1.0, 6.0, ((0, 4), (1, 16), (2, 4)))
    w_gate = centred(key_list[7], (SECTIONS, EXPERTS, D, HIDDEN_SIZE), D ** -0.5, 0.09375, ((0, 4), (1, 16), (3, 4)))
    w_up = centred(key_list[8], (SECTIONS, EXPERTS, D, HIDDEN_SIZE), D ** -0.5, 0.09375, ((0, 4), (1, 16), (3, 4)))
    w_down = centred(key_list[9], (SECTIONS, EXPERTS, HIDDEN_SIZE, D), HIDDEN_SIZE ** -0.5, 0.125, ((0, 4), (1, 16), (2, 4)))
    return {"x_fwd": x_fwd, "ids_fwd": ids_fwd, "gates_fwd": gates_fwd, "x_bwd": x_bwd, "ids_bwd": ids_bwd, "gates_bwd": gates_bwd, "grad_in": grad_in, "w_gate": w_gate, "w_up": w_up, "w_down": w_down}


def group_sum(left, right_fn, groups):
    part = HIDDEN_SIZE // groups
    total = None
    for group in range(groups):
        piece = right_fn(left, group * part, part).astype(jnp.bfloat16)
        piece = lax.optimization_barrier(piece).astype(jnp.float32)
        total = piece if total is None else total + piece
    return total.astype(jnp.bfloat16)


def forward_section(x_rows, route_ids, gate_vals, w_gate, w_up, w_down):
    limit = N_EXPERT * CAP

    def per_expert(total, inputs):
        which, gate_mat, up_mat, down_mat = inputs
        match = route_ids == which
        hit = jnp.any(match, axis=1)
        weight = jnp.sum(jnp.where(match, gate_vals, 0.0), axis=1)
        order = jnp.argsort(jnp.where(hit, 0, 1).astype(jnp.int32), stable=True)[:limit]
        rows = x_rows[order]
        gate_pre = jnp.dot(rows, gate_mat, preferred_element_type=jnp.float32)
        up_pre = jnp.dot(rows, up_mat, preferred_element_type=jnp.float32)
        hidden = (jax.nn.silu(gate_pre) * up_pre).astype(jnp.bfloat16)

        def down_part(left, start, part):
            return jnp.dot(left[:, start:start + part], down_mat[start:start + part], preferred_element_type=jnp.float32)

        out_rows = group_sum(hidden, down_part, N_DP)
        contrib = jnp.where(hit[order][:, None], weight[order][:, None] * out_rows.astype(jnp.float32), 0.0)
        return total.at[order].add(contrib), None

    start_total = jnp.zeros(x_rows.shape, jnp.float32)
    indices = jnp.arange(EXPERTS, dtype=jnp.int32)
    total, _ = lax.scan(per_expert, start_total, (indices, w_gate, w_up, w_down))
    return (x_rows.astype(jnp.float32) + total).astype(jnp.bfloat16)


def backward_section(x_rows, route_ids, gate_vals, grad_rows, w_gate, w_up, w_down):
    limit = N_EXPERT * CAP

    def per_expert(total, inputs):
        which, gate_mat, up_mat, down_mat = inputs
        match = route_ids == which
        hit = jnp.any(match, axis=1)
        weight = jnp.sum(jnp.where(match, gate_vals, 0.0), axis=1)
        order = jnp.argsort(jnp.where(hit, 0, 1).astype(jnp.int32), stable=True)[:limit]
        rows = x_rows[order]
        scaled = (weight[order][:, None] * grad_rows[order].astype(jnp.float32)).astype(jnp.bfloat16)
        gate_pre = jnp.dot(rows, gate_mat, preferred_element_type=jnp.float32)
        up_pre = jnp.dot(rows, up_mat, preferred_element_type=jnp.float32)
        squash = jax.nn.sigmoid(gate_pre)
        back_hidden = jnp.dot(scaled, down_mat.T, preferred_element_type=jnp.float32)
        d_gate = (back_hidden * up_pre * squash * (1.0 + gate_pre * (1.0 - squash))).astype(jnp.bfloat16)
        d_up = (back_hidden * gate_pre * squash).astype(jnp.bfloat16)

        def input_part(left, start, part):
            first = jnp.dot(left[0][:, start:start + part], gate_mat[:, start:start + part].T, preferred_element_type=jnp.float32)
            second = jnp.dot(left[1][:, start:start + part], up_mat[:, start:start + part].T, preferred_element_type=jnp.float32)
            return first + second

        grad_part = group_sum((d_gate, d_up), input_part, N_DP)
        contrib = jnp.where(hit[order][:, None], grad_part.astype(jnp.float32), 0.0)
        return total.at[order].add(contrib), None

    start_total = jnp.zeros(x_rows.shape, jnp.float32)
    indices = jnp.arange(EXPERTS, dtype=jnp.int32)
    total, _ = lax.scan(per_expert, start_total, (indices, w_gate, w_up, w_down))
    return (grad_rows.astype(jnp.float32) + total).astype(jnp.bfloat16)


def reference(x_fwd, ids_fwd, gates_fwd, x_bwd, ids_bwd, gates_bwd, grad_in, w_gate, w_up, w_down):
    outputs = []
    grads = []
    for section in range(SECTIONS):
        outputs.append(forward_section(x_fwd[section], ids_fwd[section], gates_fwd[section], w_gate[section], w_up[section], w_down[section]))
        grads.append(backward_section(x_bwd[section], ids_bwd[section], gates_bwd[section], grad_in[section], w_gate[section], w_up[section], w_down[section]))
    layer_out = jnp.stack(outputs)
    layer_grad = jnp.stack(grads)
    return jnp.roll(layer_out, 1, axis=0), jnp.roll(layer_grad, -1, axis=0)
```

```python
import functools

import jax
import jax.numpy as jnp
from jax import lax
from jax.experimental import pallas as pl
from jax.experimental.pallas import tpu as pltpu
from jax.sharding import PartitionSpec as P

F32 = jnp.float32
BF16 = jnp.bfloat16
MIB = 1024 * 1024


def shifted(array, axis, by):
    count = lax.axis_size(axis)
    return lax.ppermute(array, axis, [(i, (i + by) % count) for i in range(count)])


def dot(a, b):
    return jnp.dot(a, b, preferred_element_type=F32)


def dot_nt(a, b):
    return lax.dot_general(a, b, (((1,), (1,)), ((), ())), preferred_element_type=F32)


def params(mib):
    return pltpu.CompilerParams(vmem_limit_bytes=mib * MIB)


def cost(flops, nbytes):
    return pl.CostEstimate(flops=int(flops), bytes_accessed=int(nbytes), transcendentals=0)


def whole(shape):
    return pl.BlockSpec(shape, lambda *_: (0,) * len(shape))


def targets(ids, experts, capacity):
    topk, rows = ids.shape
    expert_of = lax.broadcasted_iota(jnp.int32, (experts, rows), 0)
    earlier = (
        lax.broadcasted_iota(jnp.int32, (rows, rows), 0)
        < lax.broadcasted_iota(jnp.int32, (rows, rows), 1)
    ).astype(BF16)
    before = jnp.zeros((experts, 1), F32)
    found = []
    for k in range(topk):
        named = (expert_of == ids[k : k + 1]).astype(F32)
        place = dot(named.astype(BF16), earlier) + before
        place = jnp.sum(named * place, axis=0, keepdims=True)
        found.append(ids[k : k + 1] * capacity + place.astype(jnp.int32))
        before = before + jnp.sum(named, axis=1, keepdims=True)
    return found


def as_column(row):
    rows = row.shape[1]
    same = lax.broadcasted_iota(jnp.int32, (rows, rows), 0) == lax.broadcasted_iota(
        jnp.int32, (rows, rows), 1
    )
    return jnp.sum(jnp.where(same, row, jnp.zeros_like(row)), axis=1, keepdims=True)


def slot_hits(ids, experts, capacity):
    rows = ids.shape[1]
    slot = lax.broadcasted_iota(jnp.int32, (experts * capacity, rows), 0)
    return [slot == t for t in targets(ids, experts, capacity)]


def one_hot(hit):
    return jnp.where(hit, 1.0, 0.0).astype(BF16)


def pack_kernel(experts, capacity, rank_ref, ids_ref, source_ref, out_ref):
    hits = slot_hits(ids_ref[...], experts, capacity)
    chosen = one_hot(functools.reduce(jnp.logical_or, hits))
    out_ref[...] = dot(chosen, source_ref[...]).astype(BF16)


def pack_scaled_kernel(experts, capacity, ids_ref, gates_ref, source_ref, out_ref):
    hits = slot_hits(ids_ref[...], experts, capacity)
    chosen = one_hot(functools.reduce(jnp.logical_or, hits))
    gate = sum(
        jnp.sum(jnp.where(hit, gates_ref[k : k + 1], 0.0), axis=1, keepdims=True)
        for k, hit in enumerate(hits)
    )
    out_ref[...] = (gate * dot(chosen, source_ref[...])).astype(BF16)


def pack(rank, ids, source, experts, capacity, quarter):
    rows = source.shape[0]
    slots = experts * capacity
    return pl.pallas_call(
        functools.partial(pack_kernel, experts, capacity),
        grid_spec=pltpu.PrefetchScalarGridSpec(
            num_scalar_prefetch=1,
            grid=(1,),
            in_specs=[
                whole(ids.shape),
                pl.BlockSpec((rows, quarter), lambda i, order: (0, order[0])),
            ],
            out_specs=whole((slots, quarter)),
        ),
        out_shape=jax.ShapeDtypeStruct((slots, quarter), BF16),
        compiler_params=params(24),
        cost_estimate=cost(2 * slots * rows * quarter, 4 * slots * quarter),
    )(rank, ids, source)


def pack_scaled(ids, gates, source, experts, capacity):
    rows, quarter = source.shape
    slots = experts * capacity
    return pl.pallas_call(
        functools.partial(pack_scaled_kernel, experts, capacity),
        out_shape=jax.ShapeDtypeStruct((slots, quarter), BF16),
        compiler_params=params(24),
        cost_estimate=cost(2 * slots * rows * quarter, 4 * slots * quarter),
    )(ids, gates, source)


def token_hits(ids, experts, capacity):
    rows = ids.shape[1]
    slot = lax.broadcasted_iota(jnp.int32, (rows, experts * capacity), 1)
    return [slot == as_column(t) for t in targets(ids, experts, capacity)]


def combine_gated_kernel(experts, capacity, rank_ref, ids_ref, gates_ref, own_ref, back_ref, out_ref):
    total = own_ref[...].astype(F32)
    for k, hit in enumerate(token_hits(ids_ref[...], experts, capacity)):
        total += as_column(gates_ref[k : k + 1]) * dot(one_hot(hit), back_ref[...])
    out_ref[...] = total.astype(BF16)


def combine_kernel(experts, capacity, ids_ref, own_ref, back_ref, out_ref):
    hits = token_hits(ids_ref[...], experts, capacity)
    chosen = one_hot(functools.reduce(jnp.logical_or, hits))
    total = own_ref[...].astype(F32) + dot(chosen, back_ref[...])
    out_ref[...] = total.astype(BF16)


def combine_gated(rank, ids, gates, own, back, experts, capacity):
    rows = ids.shape[1]
    slots, quarter = back.shape
    return pl.pallas_call(
        functools.partial(combine_gated_kernel, experts, capacity),
        grid_spec=pltpu.PrefetchScalarGridSpec(
            num_scalar_prefetch=1,
            grid=(1,),
            in_specs=[
                whole(ids.shape),
                whole(gates.shape),
                pl.BlockSpec((rows, quarter), lambda i, order: (0, order[0])),
                whole(back.shape),
            ],
            out_specs=whole((rows, quarter)),
        ),
        out_shape=jax.ShapeDtypeStruct((rows, quarter), BF16),
        compiler_params=params(24),
        cost_estimate=cost(4 * slots * rows * quarter, 4 * slots * quarter),
    )(rank, ids, gates, own, back)


def combine(ids, own, back, experts, capacity):
    rows = ids.shape[1]
    slots, quarter = back.shape
    return pl.pallas_call(
        functools.partial(combine_kernel, experts, capacity),
        out_shape=jax.ShapeDtypeStruct((rows, quarter), BF16),
        compiler_params=params(24),
        cost_estimate=cost(2 * slots * rows * quarter, 4 * slots * quarter),
    )(ids, own, back)


def gather_quarters(block):
    half = block.shape[0] // 2
    left = shifted(block, "dp", 1)
    right = shifted(block, "dp", -1)
    far_top = shifted(left[:half], "dp", 1)
    far_bottom = shifted(right[half:], "dp", -1)
    return (block, left, right, far_top, far_bottom)


def pick(step, refs, far_ref):
    own, left, right, far_top, far_bottom = refs
    half = far_top.shape[0]

    @pl.when(step == 0)
    def _():
        far_ref[...] = own[...]

    @pl.when(step == 1)
    def _():
        far_ref[...] = left[...]

    @pl.when(step == 2)
    def _():
        far_ref[...] = right[...]

    @pl.when(step == 3)
    def _():
        far_ref[:half] = far_top[...]
        far_ref[half:] = far_bottom[...]

    return far_ref[...]


def forward_hidden_kernel(order_ref, *refs):
    xs = refs[:5]
    gate_ref, up_ref, down_ref, hidden_ref, far_out_ref, rows_ref, gate_acc, up_acc = refs[5:]
    step = pl.program_id(0)
    rows = pick(step, xs, rows_ref)
    gate_part = dot(rows, gate_ref[...])
    up_part = dot(rows, up_ref[...])

    @pl.when(step == 0)
    def _():
        gate_acc[...] = gate_part
        up_acc[...] = up_part

    @pl.when(step > 0)
    def _():
        gate_acc[...] += gate_part
        up_acc[...] += up_part

    @pl.when(step == pl.num_programs(0) - 1)
    def _():
        gate_pre = gate_acc[...]
        hidden = (gate_pre * jax.nn.sigmoid(gate_pre) * up_acc[...]).astype(BF16)
        hidden_ref[...] = hidden
        far_out_ref[...] = dot(hidden, down_ref[...]).astype(BF16)


def quarter_specs(blocks):
    return [
        pl.BlockSpec(b.shape, lambda i, order: (0, 0), pipeline_mode=pl.Buffered(1)) for b in blocks
    ]


def forward_hidden(order, xs, gate_mat, up_mat, down_mat):
    slots, quarter = xs[0].shape
    width = gate_mat.shape[1]
    groups = gate_mat.shape[0] // quarter
    weight = pl.BlockSpec((quarter, width), lambda i, order: (order[i], 0))
    return pl.pallas_call(
        forward_hidden_kernel,
        grid_spec=pltpu.PrefetchScalarGridSpec(
            num_scalar_prefetch=1,
            grid=(groups,),
            in_specs=quarter_specs(xs)
            + [weight, weight, pl.BlockSpec((width, quarter), lambda i, order: (0, order[3]))],
            out_specs=[whole((slots, width)), whole((slots, quarter))],
            scratch_shapes=[
                pltpu.VMEM((slots, quarter), BF16),
                pltpu.VMEM((slots, width), F32),
                pltpu.VMEM((slots, width), F32),
            ],
        ),
        out_shape=[
            jax.ShapeDtypeStruct((slots, width), BF16),
            jax.ShapeDtypeStruct((slots, quarter), BF16),
        ],
        compiler_params=params(40),
        cost_estimate=cost(
            2 * slots * width * quarter * (2 * groups + 1), 2 * quarter * width * (2 * groups + 1)
        ),
    )(order, *xs, gate_mat, up_mat, down_mat)


def forward_rest_kernel(order_ref, hidden_ref, down_ref, *out_refs):
    step = pl.program_id(0)
    part = dot(hidden_ref[...], down_ref[...]).astype(BF16)
    for number, out_ref in enumerate(out_refs):

        @pl.when(step == number)
        def _():
            out_ref[...] = part


def forward_rest(order, hidden, down_mat, quarter):
    slots, width = hidden.shape
    return pl.pallas_call(
        forward_rest_kernel,
        grid_spec=pltpu.PrefetchScalarGridSpec(
            num_scalar_prefetch=1,
            grid=(3,),
            in_specs=[
                whole((slots, width)),
                pl.BlockSpec((width, quarter), lambda i, order: (0, order[(i + 1) % 3])),
            ],
            out_specs=[whole((slots, quarter))] * 3,
        ),
        out_shape=[jax.ShapeDtypeStruct((slots, quarter), BF16)] * 3,
        compiler_params=params(40),
        cost_estimate=cost(6 * slots * width * quarter, 6 * quarter * (width + slots)),
    )(order, hidden, down_mat)


def backward_hidden_kernel(order_ref, *refs):
    ss, xs = refs[:5], refs[5:10]
    (
        gate_ref,
        up_ref,
        down_ref,
        far_gate_ref,
        far_up_ref,
        d_gate_ref,
        d_up_ref,
        far_out_ref,
        rows_ref,
        gate_acc,
        up_acc,
        back_acc,
    ) = refs[10:]
    step = pl.program_id(0)
    rows = pick(step, xs, rows_ref)
    gate_part = dot(rows, gate_ref[...])
    up_part = dot(rows, up_ref[...])
    scaled = pick(step, ss, rows_ref)
    back_part = dot_nt(scaled, down_ref[...])

    @pl.when(step == 0)
    def _():
        gate_acc[...] = gate_part
        up_acc[...] = up_part
        back_acc[...] = back_part

    @pl.when(step > 0)
    def _():
        gate_acc[...] += gate_part
        up_acc[...] += up_part
        back_acc[...] += back_part

    @pl.when(step == pl.num_programs(0) - 1)
    def _():
        gate_pre = gate_acc[...]
        squash = jax.nn.sigmoid(gate_pre)
        turned = back_acc[...] * squash
        d_gate = (turned * up_acc[...] * (1.0 + gate_pre * (1.0 - squash))).astype(BF16)
        d_up = (turned * gate_pre).astype(BF16)
        d_gate_ref[...] = d_gate
        d_up_ref[...] = d_up
        far = dot_nt(d_gate, far_gate_ref[...]) + dot_nt(d_up, far_up_ref[...])
        far_out_ref[...] = far.astype(BF16)


def backward_hidden(order, ss, xs, gate_mat, up_mat, down_mat):
    slots, quarter = xs[0].shape
    width = gate_mat.shape[1]
    groups = gate_mat.shape[0] // quarter
    weight = pl.BlockSpec((quarter, width), lambda i, order: (order[i], 0))
    far = pl.BlockSpec((quarter, width), lambda i, order: (order[3], 0))
    return pl.pallas_call(
        backward_hidden_kernel,
        grid_spec=pltpu.PrefetchScalarGridSpec(
            num_scalar_prefetch=1,
            grid=(groups,),
            in_specs=quarter_specs(ss)
            + quarter_specs(xs)
            + [
                weight,
                weight,
                pl.BlockSpec((width, quarter), lambda i, order: (0, order[i])),
                far,
                far,
            ],
            out_specs=[whole((slots, width)), whole((slots, width)), whole((slots, quarter))],
            scratch_shapes=[pltpu.VMEM((slots, quarter), BF16)]
            + [pltpu.VMEM((slots, width), F32)] * 3,
        ),
        out_shape=[
            jax.ShapeDtypeStruct((slots, width), BF16),
            jax.ShapeDtypeStruct((slots, width), BF16),
            jax.ShapeDtypeStruct((slots, quarter), BF16),
        ],
        compiler_params=params(48),
        cost_estimate=cost(
            2 * slots * width * quarter * (3 * groups + 2), 2 * quarter * width * (3 * groups + 2)
        ),
    )(order, *ss, *xs, gate_mat, up_mat, down_mat, gate_mat, up_mat)


def backward_rest_kernel(order_ref, d_gate_ref, d_up_ref, gate_ref, up_ref, *out_refs):
    step = pl.program_id(0)
    part = dot_nt(d_gate_ref[...], gate_ref[...]) + dot_nt(d_up_ref[...], up_ref[...])
    part = part.astype(BF16)
    for number, out_ref in enumerate(out_refs):

        @pl.when(step == number)
        def _():
            out_ref[...] = part


def backward_rest(order, d_gate, d_up, gate_mat, up_mat, quarter):
    slots, width = d_gate.shape
    weight = pl.BlockSpec((quarter, width), lambda i, order: (order[(i + 1) % 3], 0))
    return pl.pallas_call(
        backward_rest_kernel,
        grid_spec=pltpu.PrefetchScalarGridSpec(
            num_scalar_prefetch=1,
            grid=(3,),
            in_specs=[whole((slots, width)), whole((slots, width)), weight, weight],
            out_specs=[whole((slots, quarter))] * 3,
        ),
        out_shape=[jax.ShapeDtypeStruct((slots, quarter), BF16)] * 3,
        compiler_params=params(40),
        cost_estimate=cost(12 * slots * width * quarter, 6 * quarter * (2 * width + slots)),
    )(order, d_gate, d_up, gate_mat, up_mat)


def relay_add_kernel(left_ref, right_ref, top_ref, bottom_ref, left_out, right_out):
    half = top_ref.shape[0]
    left_out[:half] = (left_ref[:half].astype(F32) + top_ref[...].astype(F32)).astype(BF16)
    left_out[half:] = left_ref[half:]
    right_out[:half] = right_ref[:half]
    right_out[half:] = (right_ref[half:].astype(F32) + bottom_ref[...].astype(F32)).astype(BF16)


def relay_add(left, right, top, bottom):
    shape = jax.ShapeDtypeStruct(left.shape, BF16)
    return pl.pallas_call(
        relay_add_kernel,
        out_shape=[shape, shape],
        compiler_params=params(24),
        cost_estimate=cost(left.size, 10 * left.size),
    )(left, right, top, bottom)


def sum_kernel(a_ref, b_ref, c_ref, out_ref):
    total = a_ref[...].astype(F32) + b_ref[...].astype(F32) + c_ref[...].astype(F32)
    out_ref[...] = total.astype(BF16)


def summed(a, b, c):
    return pl.pallas_call(
        sum_kernel,
        out_shape=jax.ShapeDtypeStruct(a.shape, BF16),
        compiler_params=params(24),
        cost_estimate=cost(3 * a.size, 8 * a.size),
    )(a, b, c)


def far_halves(far):
    half = far.shape[0] // 2
    return shifted(far[:half], "dp", -1), shifted(far[half:], "dp", 1)


def scatter_sums(left, right, own, top, bottom):
    to_left, to_right = relay_add(left, right, top, bottom)
    return summed(own, shifted(to_left, "dp", -1), shifted(to_right, "dp", 1))


def exchange(rows, experts):
    slots, width = rows.shape
    blocks = rows.reshape(experts, slots // experts, width)
    return lax.all_to_all(blocks, "expert", split_axis=0, concat_axis=0, tiled=True).reshape(
        slots, width
    )


def local(x_fwd, ids_fwd, gates_fwd, x_bwd, ids_bwd, gates_bwd, grad_in, w_gate, w_up, w_down):
    experts = lax.axis_size("expert")
    groups = lax.axis_size("dp")
    dp_rank = lax.axis_index("dp")
    rows_dev = x_fwd.shape[1]
    topk = ids_fwd.shape[2]
    capacity = rows_dev * topk * 3 // (2 * experts)
    quarter = x_fwd.shape[2] // groups
    order = (dp_rank + jnp.array([0, groups - 1, 1, 2], jnp.int32)) % groups
    gate_mat = w_gate[0, 0]
    up_mat = w_up[0, 0]
    down_mat = w_down[0, 0]
    fwd_ids, fwd_gates = ids_fwd[0].T, gates_fwd[0].T
    bwd_ids, bwd_gates = ids_bwd[0].T, gates_bwd[0].T

    scaled = pack_scaled(bwd_ids, bwd_gates, grad_in[0], experts, capacity)
    scaled = exchange(scaled, experts)
    bwd_rows = exchange(pack(order, bwd_ids, x_bwd[0], experts, capacity, quarter), experts)
    fwd_rows = exchange(pack(order, fwd_ids, x_fwd[0], experts, capacity, quarter), experts)

    ss = gather_quarters(scaled)
    xs = gather_quarters(bwd_rows)
    fs = gather_quarters(fwd_rows)

    d_gate, d_up, far = backward_hidden(order, ss, xs, gate_mat, up_mat, down_mat)
    top, bottom = far_halves(far)
    left, right, own = backward_rest(order, d_gate, d_up, gate_mat, up_mat, quarter)
    bwd_sum = scatter_sums(left, right, own, top, bottom)
    bwd_back = exchange(bwd_sum, experts)

    hidden, far = forward_hidden(order, fs, gate_mat, up_mat, down_mat)
    top, bottom = far_halves(far)
    left, right, own = forward_rest(order, hidden, down_mat, quarter)
    fwd_sum = scatter_sums(left, right, own, top, bottom)
    fwd_back = exchange(fwd_sum, experts)

    layer_grad = combine(bwd_ids, grad_in[0], bwd_back, experts, capacity)
    sent_backward = shifted(layer_grad[None], "pipe", -1)
    layer_out = combine_gated(order, fwd_ids, fwd_gates, x_fwd[0], fwd_back, experts, capacity)
    sent_forward = shifted(layer_out[None], "pipe", 1)
    return (sent_forward, sent_backward)


def solution(mesh):
    in_specs = (
        P("pipe", "expert", None),
        P("pipe", "expert", None),
        P("pipe", "expert", None),
        P("pipe", "expert", None),
        P("pipe", "expert", None),
        P("pipe", "expert", None),
        P("pipe", "expert", "dp"),
        P("pipe", "expert", None, "dp"),
        P("pipe", "expert", None, "dp"),
        P("pipe", "expert", "dp", None),
    )
    out_specs = (P("pipe", "expert", "dp"), P("pipe", "expert", "dp"))
    return jax.shard_map(local, mesh=mesh, in_specs=in_specs, out_specs=out_specs, check_vma=False)
```

```python
import functools

import jax
import jax.numpy as jnp
from jax import lax
from jax.experimental import pallas as pl
from jax.experimental.pallas import tpu as pltpu
from jax.sharding import PartitionSpec as P

F32 = jnp.float32
BF16 = jnp.bfloat16
MIB = 1024 * 1024


def shifted(array, axis, by):
    count = lax.axis_size(axis)
    return lax.ppermute(array, axis, [(i, (i + by) % count) for i in range(count)])


def dot(a, b):
    return jnp.dot(a, b, preferred_element_type=F32)


def dot_nt(a, b):
    return lax.dot_general(a, b, (((1,), (1,)), ((), ())), preferred_element_type=F32)


def params(mib):
    return pltpu.CompilerParams(vmem_limit_bytes=mib * MIB)


def cost(flops, nbytes):
    return pl.CostEstimate(flops=int(flops), bytes_accessed=int(nbytes), transcendentals=0)


def lasting(microseconds):
    return pl.CostEstimate(flops=int(1e9 * microseconds), bytes_accessed=0, transcendentals=0)


def whole(shape):
    return pl.BlockSpec(shape, lambda *_: (0,) * len(shape))


def targets(ids, experts, capacity):
    topk, rows = ids.shape
    expert_of = lax.broadcasted_iota(jnp.int32, (experts, rows), 0)
    earlier = (
        lax.broadcasted_iota(jnp.int32, (rows, rows), 0)
        < lax.broadcasted_iota(jnp.int32, (rows, rows), 1)
    ).astype(BF16)
    before = jnp.zeros((experts, 1), F32)
    found = []
    for k in range(topk):
        named = (expert_of == ids[k : k + 1]).astype(F32)
        place = dot(named.astype(BF16), earlier) + before
        place = jnp.sum(named * place, axis=0, keepdims=True)
        found.append(ids[k : k + 1] * capacity + place.astype(jnp.int32))
        before = before + jnp.sum(named, axis=1, keepdims=True)
    return found


def as_column(row):
    rows = row.shape[1]
    same = lax.broadcasted_iota(jnp.int32, (rows, rows), 0) == lax.broadcasted_iota(
        jnp.int32, (rows, rows), 1
    )
    return jnp.sum(jnp.where(same, row, jnp.zeros_like(row)), axis=1, keepdims=True)


def slot_hits(ids, experts, capacity):
    rows = ids.shape[1]
    slot = lax.broadcasted_iota(jnp.int32, (experts * capacity, rows), 0)
    return [slot == t for t in targets(ids, experts, capacity)]


def one_hot(hit):
    return jnp.where(hit, 1.0, 0.0).astype(BF16)


def pack_kernel(experts, capacity, ids_ref, source_ref, out_ref):
    hits = slot_hits(ids_ref[...], experts, capacity)
    chosen = one_hot(functools.reduce(jnp.logical_or, hits))
    out_ref[...] = dot(chosen, source_ref[...]).astype(BF16)


def pack(ids, source, experts, capacity):
    slots, width = experts * capacity, source.shape[1]
    return pl.pallas_call(
        functools.partial(pack_kernel, experts, capacity),
        out_shape=jax.ShapeDtypeStruct((slots, width), BF16),
        compiler_params=params(32),
        cost_estimate=cost(2 * slots * source.size, 4 * slots * width),
    )(ids, source)


def pack_pair_kernel(experts, capacity, order_ref, ids_ref, gates_ref, grad_ref, source_ref, out_ref):
    hits = slot_hits(ids_ref[...], experts, capacity)
    chosen = one_hot(functools.reduce(jnp.logical_or, hits))
    gate = sum(
        jnp.sum(jnp.where(hit, gates_ref[k : k + 1], 0.0), axis=1, keepdims=True)
        for k, hit in enumerate(hits)
    )
    quarter = grad_ref.shape[1]
    out_ref[:, :quarter] = (gate * dot(chosen, grad_ref[...])).astype(BF16)
    out_ref[:, quarter:] = dot(chosen, source_ref[...]).astype(BF16)


def pack_pair(order, ids, gates, grad, source, experts, capacity):
    rows, quarter = grad.shape
    slots = experts * capacity
    return pl.pallas_call(
        functools.partial(pack_pair_kernel, experts, capacity),
        grid_spec=pltpu.PrefetchScalarGridSpec(
            num_scalar_prefetch=1,
            grid=(1,),
            in_specs=[
                whole(ids.shape),
                whole(gates.shape),
                whole(grad.shape),
                pl.BlockSpec((rows, quarter), lambda i, order: (0, order[0])),
            ],
            out_specs=whole((slots, 2 * quarter)),
        ),
        out_shape=jax.ShapeDtypeStruct((slots, 2 * quarter), BF16),
        compiler_params=params(60),
        cost_estimate=cost(4 * slots * rows * quarter, 8 * slots * quarter),
    )(order, ids, gates, grad, source)


def token_hits(ids, experts, capacity):
    rows = ids.shape[1]
    slot = lax.broadcasted_iota(jnp.int32, (rows, experts * capacity), 1)
    return [slot == as_column(t) for t in targets(ids, experts, capacity)]


def combine_gated_kernel(experts, capacity, rank_ref, ids_ref, gates_ref, own_ref, back_ref, out_ref):
    total = own_ref[...].astype(F32)
    for k, hit in enumerate(token_hits(ids_ref[...], experts, capacity)):
        total += as_column(gates_ref[k : k + 1]) * dot(one_hot(hit), back_ref[...])
    out_ref[...] = total.astype(BF16)


def combine_kernel(experts, capacity, ids_ref, own_ref, back_ref, out_ref):
    hits = token_hits(ids_ref[...], experts, capacity)
    chosen = one_hot(functools.reduce(jnp.logical_or, hits))
    total = own_ref[...].astype(F32) + dot(chosen, back_ref[...])
    out_ref[...] = total.astype(BF16)


def combine_gated(rank, ids, gates, own, back, experts, capacity):
    rows = ids.shape[1]
    slots, quarter = back.shape
    return pl.pallas_call(
        functools.partial(combine_gated_kernel, experts, capacity),
        grid_spec=pltpu.PrefetchScalarGridSpec(
            num_scalar_prefetch=1,
            grid=(1,),
            in_specs=[
                whole(ids.shape),
                whole(gates.shape),
                pl.BlockSpec((rows, quarter), lambda i, order: (0, order[0])),
                whole(back.shape),
            ],
            out_specs=whole((rows, quarter)),
        ),
        out_shape=jax.ShapeDtypeStruct((rows, quarter), BF16),
        compiler_params=params(24),
        cost_estimate=cost(4 * slots * rows * quarter, 4 * slots * quarter),
    )(rank, ids, gates, own, back)


def combine(ids, own, back, experts, capacity):
    rows = ids.shape[1]
    slots, quarter = back.shape
    return pl.pallas_call(
        functools.partial(combine_kernel, experts, capacity),
        out_shape=jax.ShapeDtypeStruct((rows, quarter), BF16),
        compiler_params=params(24),
        cost_estimate=cost(2 * slots * rows * quarter, 4 * slots * quarter),
    )(ids, own, back)


def halves_kernel(top_ref, bottom_ref, top_out, bottom_out):
    top_out[...] = top_ref[...]
    bottom_out[...] = bottom_ref[...]


def halves(first, second):
    rows, width = first.shape
    half = (rows // 2, width)
    shape = jax.ShapeDtypeStruct(half, BF16)
    return pl.pallas_call(
        halves_kernel,
        grid=(1,),
        in_specs=[
            pl.BlockSpec(half, lambda i: (0, 0)),
            pl.BlockSpec(half, lambda i: (1, 0)),
        ],
        out_specs=[whole(half)] * 2,
        out_shape=[shape, shape],
        compiler_params=params(24),
        cost_estimate=cost(rows, 4 * rows * width),
    )(first, second)


def fixed(shape):
    return pl.BlockSpec(shape, lambda *_: (0,) * len(shape), pipeline_mode=pl.Buffered(1))


def accumulate(step, acc_ref, part):
    @pl.when(step == 0)
    def _():
        acc_ref[...] = part

    @pl.when(step > 0)
    def _():
        acc_ref[...] += part


def backward_early_kernel(order_ref, own, left, right, gate_ref, up_ref, down_ref, *refs):
    gate_acc, up_acc, back_acc, rows_ref = refs
    step = pl.program_id(0)
    for number, ref in enumerate((own, left, right)):

        @pl.when(step == number)
        def _():
            rows_ref[...] = ref[...]

    quarter = rows_ref.shape[1] // 2
    accumulate(step, back_acc, dot_nt(rows_ref[:, :quarter], down_ref[...]))
    accumulate(step, gate_acc, dot(rows_ref[:, quarter:], gate_ref[...]))
    accumulate(step, up_acc, dot(rows_ref[:, quarter:], up_ref[...]))


def backward_early(order, blocks, gate_mat, up_mat, down_mat):
    slots, pair = blocks[0].shape
    width, quarter = down_mat.shape[0], pair // 2
    weight = pl.BlockSpec((quarter, width), lambda i, order: (order[i], 0))
    return pl.pallas_call(
        backward_early_kernel,
        grid_spec=pltpu.PrefetchScalarGridSpec(
            num_scalar_prefetch=1,
            grid=(3,),
            in_specs=[fixed(b.shape) for b in blocks]
            + [weight, weight, pl.BlockSpec((width, quarter), lambda i, order: (0, order[i]))],
            out_specs=[whole((slots, width))] * 3,
            scratch_shapes=[pltpu.VMEM((slots, pair), BF16)],
        ),
        out_shape=[jax.ShapeDtypeStruct((slots, width), F32)] * 3,
        compiler_params=params(32),
        cost_estimate=cost(18 * slots * width * quarter, 18 * quarter * width),
    )(order, *blocks, gate_mat, up_mat, down_mat)


def split(value, top_out, bottom_out):
    half = top_out.shape[0]
    top_out[...] = value[:half].astype(BF16)
    bottom_out[...] = value[half:].astype(BF16)


def backward_late_kernel(order_ref, top, bottom, gate_in, up_in, back_in, gate_ref, up_ref, down_ref, *refs):
    d_gate_ref, d_up_ref, top_out, bottom_out, rows_ref = refs
    half = top.shape[0]
    quarter = rows_ref.shape[1] // 2
    rows_ref[:half] = top[...]
    rows_ref[half:] = bottom[...]
    gate_pre = gate_in[...] + dot(rows_ref[:, quarter:], gate_ref[...])
    up_pre = up_in[...] + dot(rows_ref[:, quarter:], up_ref[...])
    back = back_in[...] + dot_nt(rows_ref[:, :quarter], down_ref[...])
    squash = jax.nn.sigmoid(gate_pre)
    turned = back * squash
    d_gate = (turned * up_pre * (1.0 + gate_pre * (1.0 - squash))).astype(BF16)
    d_up = (turned * gate_pre).astype(BF16)
    d_gate_ref[...] = d_gate
    d_up_ref[...] = d_up
    split(dot_nt(d_gate, gate_ref[...]) + dot_nt(d_up, up_ref[...]), top_out, bottom_out)


def backward_late(order, far, accs, gate_mat, up_mat, down_mat):
    half, pair = far[0].shape
    quarter = pair // 2
    slots, width = accs[0].shape
    rows = pl.BlockSpec((quarter, width), lambda i, order: (order[3], 0))
    columns = pl.BlockSpec((width, quarter), lambda i, order: (0, order[3]))
    wide = jax.ShapeDtypeStruct((slots, width), BF16)
    part = jax.ShapeDtypeStruct((half, quarter), BF16)
    return pl.pallas_call(
        backward_late_kernel,
        grid_spec=pltpu.PrefetchScalarGridSpec(
            num_scalar_prefetch=1,
            grid=(1,),
            in_specs=[fixed(b.shape) for b in (*far, *accs)] + [rows, rows, columns],
            out_specs=[whole(wide.shape)] * 2 + [whole(part.shape)] * 2,
            scratch_shapes=[pltpu.VMEM((slots, pair), BF16)],
        ),
        out_shape=[wide, wide, part, part],
        compiler_params=params(32),
        cost_estimate=cost(10 * slots * width * quarter, 6 * quarter * width),
    )(order, *far, *accs, gate_mat, up_mat, down_mat)


def forward_hidden_kernel(order_ref, rows_ref, gate_ref, up_ref, down_ref, *refs):
    hidden_ref, top_out, bottom_out, gate_acc, up_acc = refs
    step = pl.program_id(0)
    accumulate(step, gate_acc, dot(rows_ref[...], gate_ref[...]))
    accumulate(step, up_acc, dot(rows_ref[...], up_ref[...]))

    @pl.when(step == pl.num_programs(0) - 1)
    def _():
        gate_pre = gate_acc[...]
        hidden = (gate_pre * jax.nn.sigmoid(gate_pre) * up_acc[...]).astype(BF16)
        hidden_ref[...] = hidden
        split(dot(hidden, down_ref[...]), top_out, bottom_out)


def forward_hidden(order, rows, gate_mat, up_mat, down_mat, groups):
    slots, quarter = rows.shape[0], rows.shape[1] // groups
    width = gate_mat.shape[1]
    weight = pl.BlockSpec((quarter, width), lambda i, order: (i, 0))
    wide = jax.ShapeDtypeStruct((slots, width), BF16)
    part = jax.ShapeDtypeStruct((slots // 2, quarter), BF16)
    return pl.pallas_call(
        forward_hidden_kernel,
        grid_spec=pltpu.PrefetchScalarGridSpec(
            num_scalar_prefetch=1,
            grid=(groups,),
            in_specs=[
                pl.BlockSpec((slots, quarter), lambda i, order: (0, i)),
                weight,
                weight,
                pl.BlockSpec((width, quarter), lambda i, order: (0, order[3])),
            ],
            out_specs=[whole(wide.shape)] + [whole(part.shape)] * 2,
            scratch_shapes=[pltpu.VMEM((slots, width), F32)] * 2,
        ),
        out_shape=[wide, part, part],
        compiler_params=params(60),
        cost_estimate=cost(18 * slots * width * quarter, 18 * quarter * width),
    )(order, rows, gate_mat, up_mat, down_mat)


def forward_rest_kernel(order_ref, hidden_ref, down_ref, top_ref, bottom_ref, left, right, own):
    step = pl.program_id(0)
    half = top_ref.shape[0]
    part = dot(hidden_ref[...], down_ref[...])

    @pl.when(step == 0)
    def _():
        left[:half] = (part[:half] + top_ref[...].astype(F32)).astype(BF16)
        left[half:] = part[half:].astype(BF16)

    @pl.when(step == 1)
    def _():
        right[:half] = part[:half].astype(BF16)
        right[half:] = (part[half:] + bottom_ref[...].astype(F32)).astype(BF16)

    @pl.when(step == 2)
    def _():
        own[...] = part.astype(BF16)


def forward_rest(order, hidden, down_mat, halves_in, hint):
    slots, width = hidden.shape
    half, quarter = halves_in[0].shape
    return pl.pallas_call(
        forward_rest_kernel,
        grid_spec=pltpu.PrefetchScalarGridSpec(
            num_scalar_prefetch=1,
            grid=(3,),
            in_specs=[
                whole((slots, width)),
                pl.BlockSpec((width, quarter), lambda i, order: (0, order[(i + 1) % 3])),
                whole((half, quarter)),
                whole((half, quarter)),
            ],
            out_specs=[whole((slots, quarter))] * 3,
        ),
        out_shape=[jax.ShapeDtypeStruct((slots, quarter), BF16)] * 3,
        compiler_params=params(32),
        cost_estimate=lasting(hint),
    )(order, hidden, down_mat, *halves_in)


def backward_rest_kernel(order_ref, d_gate_ref, d_up_ref, gate_ref, up_ref, *out_refs):
    step = pl.program_id(0)
    part = dot_nt(d_gate_ref[...], gate_ref[...]) + dot_nt(d_up_ref[...], up_ref[...])
    part = part.astype(BF16)
    for number, out_ref in enumerate(out_refs):

        @pl.when(step == number)
        def _():
            out_ref[...] = part


def backward_rest(order, d_gate, d_up, gate_mat, up_mat, quarter):
    slots, width = d_gate.shape
    weight = pl.BlockSpec((quarter, width), lambda i, order: (order[(i + 1) % 3], 0))
    return pl.pallas_call(
        backward_rest_kernel,
        grid_spec=pltpu.PrefetchScalarGridSpec(
            num_scalar_prefetch=1,
            grid=(3,),
            in_specs=[whole((slots, width)), whole((slots, width)), weight, weight],
            out_specs=[whole((slots, quarter))] * 3,
        ),
        out_shape=[jax.ShapeDtypeStruct((slots, quarter), BF16)] * 3,
        compiler_params=params(32),
        cost_estimate=cost(12 * slots * width * quarter, 6 * quarter * (2 * width + slots)),
    )(order, d_gate, d_up, gate_mat, up_mat)


def relay_add_kernel(left_ref, right_ref, top_ref, bottom_ref, left_out, right_out):
    half = top_ref.shape[0]
    left_out[:half] = (left_ref[:half].astype(F32) + top_ref[...].astype(F32)).astype(BF16)
    left_out[half:] = left_ref[half:]
    right_out[:half] = right_ref[:half]
    right_out[half:] = (right_ref[half:].astype(F32) + bottom_ref[...].astype(F32)).astype(BF16)


def relay_add(left, right, top, bottom):
    shape = jax.ShapeDtypeStruct(left.shape, BF16)
    return pl.pallas_call(
        relay_add_kernel,
        out_shape=[shape, shape],
        compiler_params=params(24),
        cost_estimate=lasting(1),
    )(left, right, top, bottom)


def sum_kernel(a_ref, b_ref, c_ref, *refs):
    total = a_ref[...].astype(F32) + b_ref[...].astype(F32) + c_ref[...].astype(F32)
    refs[-1][...] = total.astype(BF16)


def summed(a, b, c, hint, after=()):
    return pl.pallas_call(
        sum_kernel,
        grid=(1,),
        in_specs=[whole(a.shape)] * 3 + [pl.BlockSpec(memory_space=pl.ANY)] * len(after),
        out_specs=whole(a.shape),
        out_shape=jax.ShapeDtypeStruct(a.shape, BF16),
        compiler_params=params(24),
        cost_estimate=lasting(hint),
    )(a, b, c, *after)


def exchange(rows, experts):
    slots, width = rows.shape
    blocks = rows.reshape(experts, slots // experts, width)
    return lax.all_to_all(blocks, "expert", split_axis=0, concat_axis=0, tiled=True).reshape(
        slots, width
    )


def local(x_fwd, ids_fwd, gates_fwd, x_bwd, ids_bwd, gates_bwd, grad_in, w_gate, w_up, w_down):
    experts = lax.axis_size("expert")
    groups = lax.axis_size("dp")
    dp_rank = lax.axis_index("dp")
    rows_dev = x_fwd.shape[1]
    topk = ids_fwd.shape[2]
    capacity = rows_dev * topk * 3 // (2 * experts)
    quarter = x_fwd.shape[2] // groups
    order = (dp_rank + jnp.array([0, groups - 1, 1, 2], jnp.int32)) % groups
    gate_mat = w_gate[0, 0]
    up_mat = w_up[0, 0]
    down_mat = w_down[0, 0]
    fwd_ids, fwd_gates = ids_fwd[0].T, gates_fwd[0].T
    bwd_ids, bwd_gates = ids_bwd[0].T, gates_bwd[0].T

    bwd_rows = pack_pair(
        order, bwd_ids, bwd_gates, grad_in[0], x_bwd[0], experts, capacity
    )
    bwd_rows = exchange(bwd_rows, experts)
    fwd_rows = exchange(pack(fwd_ids, x_fwd[0], experts, capacity), experts)

    left, right = shifted(bwd_rows, "dp", 1), shifted(bwd_rows, "dp", -1)
    top, bottom = halves(left, right)
    far = shifted(top, "dp", 1), shifted(bottom, "dp", -1)
    accs = backward_early(order, (bwd_rows, left, right), gate_mat, up_mat, down_mat)
    d_gate, d_up, top, bottom = backward_late(order, far, accs, gate_mat, up_mat, down_mat)
    bwd_far = shifted(top, "dp", -1), shifted(bottom, "dp", 1)
    bwd_left, bwd_right, bwd_own = backward_rest(order, d_gate, d_up, gate_mat, up_mat, quarter)
    bwd_left, bwd_right = relay_add(bwd_left, bwd_right, *bwd_far)
    bwd_left, bwd_right = shifted(bwd_left, "dp", -1), shifted(bwd_right, "dp", 1)

    hidden, top, bottom = forward_hidden(order, fwd_rows, gate_mat, up_mat, down_mat, groups)
    fwd_far = shifted(top, "dp", -1), shifted(bottom, "dp", 1)
    bwd_back = exchange(summed(bwd_own, bwd_left, bwd_right, 20, (top,)), experts)

    fwd_left, fwd_right, fwd_own = forward_rest(order, hidden, down_mat, fwd_far, 40)
    fwd_left, fwd_right = shifted(fwd_left, "dp", -1), shifted(fwd_right, "dp", 1)
    fwd_back = exchange(summed(fwd_own, fwd_left, fwd_right, 1), experts)

    layer_grad = combine(bwd_ids, grad_in[0], bwd_back, experts, capacity)
    sent_backward = shifted(layer_grad[None], "pipe", -1)
    layer_out = combine_gated(order, fwd_ids, fwd_gates, x_fwd[0], fwd_back, experts, capacity)
    sent_forward = shifted(layer_out[None], "pipe", 1)
    return (sent_forward, sent_backward)


def solution(mesh):
    in_specs = (
        P("pipe", "expert", None),
        P("pipe", "expert", None),
        P("pipe", "expert", None),
        P("pipe", "expert", None),
        P("pipe", "expert", None),
        P("pipe", "expert", None),
        P("pipe", "expert", "dp"),
        P("pipe", "expert", None, "dp"),
        P("pipe", "expert", None, "dp"),
        P("pipe", "expert", "dp", None),
    )
    out_specs = (P("pipe", "expert", "dp"), P("pipe", "expert", "dp"))
    return jax.shard_map(local, mesh=mesh, in_specs=in_specs, out_specs=out_specs, check_vma=False)
```

```python
import functools

import jax
import jax.numpy as jnp
from jax import lax
from jax.experimental import pallas as pl
from jax.experimental.pallas import tpu as pltpu
from jax.sharding import PartitionSpec as P

F32 = jnp.float32
BF16 = jnp.bfloat16
MIB = 1024 * 1024


def shifted(array, axis, by):
    count = lax.axis_size(axis)
    return lax.ppermute(array, axis, [(i, (i + by) % count) for i in range(count)])


def dot(a, b):
    return jnp.dot(a, b, preferred_element_type=F32)


def dot_nt(a, b):
    return lax.dot_general(a, b, (((1,), (1,)), ((), ())), preferred_element_type=F32)


def params(mib):
    return pltpu.CompilerParams(vmem_limit_bytes=mib * MIB)


def cost(flops, nbytes):
    return pl.CostEstimate(flops=int(flops), bytes_accessed=int(nbytes), transcendentals=0)


def lasting(microseconds):
    return pl.CostEstimate(flops=int(1e9 * microseconds), bytes_accessed=0, transcendentals=0)


def whole(shape):
    return pl.BlockSpec(shape, lambda *_: (0,) * len(shape))


def targets(ids, experts, capacity):
    topk, rows = ids.shape
    expert_of = lax.broadcasted_iota(jnp.int32, (experts, rows), 0)
    earlier = (
        lax.broadcasted_iota(jnp.int32, (rows, rows), 0)
        < lax.broadcasted_iota(jnp.int32, (rows, rows), 1)
    ).astype(BF16)
    before = jnp.zeros((experts, 1), F32)
    found = []
    for k in range(topk):
        named = (expert_of == ids[k : k + 1]).astype(F32)
        place = dot(named.astype(BF16), earlier) + before
        place = jnp.sum(named * place, axis=0, keepdims=True)
        found.append(ids[k : k + 1] * capacity + place.astype(jnp.int32))
        before = before + jnp.sum(named, axis=1, keepdims=True)
    return found


def as_column(row):
    rows = row.shape[1]
    same = lax.broadcasted_iota(jnp.int32, (rows, rows), 0) == lax.broadcasted_iota(
        jnp.int32, (rows, rows), 1
    )
    return jnp.sum(jnp.where(same, row, jnp.zeros_like(row)), axis=1, keepdims=True)


def slot_hits(ids, experts, capacity):
    rows = ids.shape[1]
    slot = lax.broadcasted_iota(jnp.int32, (experts * capacity, rows), 0)
    return [slot == t for t in targets(ids, experts, capacity)]


def one_hot(hit):
    return jnp.where(hit, 1.0, 0.0).astype(BF16)


def pack_kernel(experts, capacity, ids_ref, source_ref, out_ref):
    hits = slot_hits(ids_ref[...], experts, capacity)
    chosen = one_hot(functools.reduce(jnp.logical_or, hits))
    out_ref[...] = dot(chosen, source_ref[...]).astype(BF16)


def pack(ids, source, experts, capacity):
    slots, width = experts * capacity, source.shape[1]
    return pl.pallas_call(
        functools.partial(pack_kernel, experts, capacity),
        out_shape=jax.ShapeDtypeStruct((slots, width), BF16),
        compiler_params=params(32),
        cost_estimate=cost(2 * slots * source.size, 4 * slots * width),
    )(ids, source)


def pack_pair_kernel(experts, capacity, ids_ref, gates_ref, grad_ref, source_hbm, out_ref, source, sem):
    quarter = grad_ref.shape[1]
    start = pl.multiple_of(lax.axis_index("dp") * quarter, 128)
    copy = pltpu.make_async_copy(source_hbm.at[:, pl.ds(start, quarter)], source, sem)
    copy.start()
    hits = slot_hits(ids_ref[...], experts, capacity)
    chosen = one_hot(functools.reduce(jnp.logical_or, hits))
    gate = sum(
        jnp.sum(jnp.where(hit, gates_ref[k : k + 1], 0.0), axis=1, keepdims=True)
        for k, hit in enumerate(hits)
    )
    out_ref[:, :quarter] = (gate * dot(chosen, grad_ref[...])).astype(BF16)
    copy.wait()
    out_ref[:, quarter:] = dot(chosen, source[...]).astype(BF16)


def pack_pair(ids, gates, grad, source, experts, capacity):
    rows, quarter = grad.shape
    slots = experts * capacity
    return pl.pallas_call(
        functools.partial(pack_pair_kernel, experts, capacity),
        grid=(1,),
        in_specs=[
            whole(ids.shape),
            whole(gates.shape),
            whole(grad.shape),
            pl.BlockSpec(memory_space=pl.ANY),
        ],
        out_specs=whole((slots, 2 * quarter)),
        out_shape=jax.ShapeDtypeStruct((slots, 2 * quarter), BF16),
        scratch_shapes=[pltpu.VMEM((rows, quarter), BF16), pltpu.SemaphoreType.DMA],
        compiler_params=params(60),
        cost_estimate=cost(4 * slots * rows * quarter, 8 * slots * quarter),
    )(ids, gates, grad, source)


def token_hits(ids, experts, capacity):
    rows = ids.shape[1]
    slot = lax.broadcasted_iota(jnp.int32, (rows, experts * capacity), 1)
    return [slot == as_column(t) for t in targets(ids, experts, capacity)]


def combine_gated_kernel(experts, capacity, rank_ref, ids_ref, gates_ref, own_ref, back_ref, out_ref):
    total = own_ref[...].astype(F32)
    for k, hit in enumerate(token_hits(ids_ref[...], experts, capacity)):
        total += as_column(gates_ref[k : k + 1]) * dot(one_hot(hit), back_ref[...])
    out_ref[...] = total.astype(BF16)


def combine_kernel(experts, capacity, ids_ref, own_ref, back_ref, out_ref):
    hits = token_hits(ids_ref[...], experts, capacity)
    chosen = one_hot(functools.reduce(jnp.logical_or, hits))
    total = own_ref[...].astype(F32) + dot(chosen, back_ref[...])
    out_ref[...] = total.astype(BF16)


def combine_gated(rank, ids, gates, own, back, experts, capacity):
    rows = ids.shape[1]
    slots, quarter = back.shape
    return pl.pallas_call(
        functools.partial(combine_gated_kernel, experts, capacity),
        grid_spec=pltpu.PrefetchScalarGridSpec(
            num_scalar_prefetch=1,
            grid=(1,),
            in_specs=[
                whole(ids.shape),
                whole(gates.shape),
                pl.BlockSpec((rows, quarter), lambda i, order: (0, order[0])),
                whole(back.shape),
            ],
            out_specs=whole((rows, quarter)),
        ),
        out_shape=jax.ShapeDtypeStruct((rows, quarter), BF16),
        compiler_params=params(24),
        cost_estimate=cost(4 * slots * rows * quarter, 4 * slots * quarter),
    )(rank, ids, gates, own, back)


def combine(ids, own, back, experts, capacity):
    rows = ids.shape[1]
    slots, quarter = back.shape
    return pl.pallas_call(
        functools.partial(combine_kernel, experts, capacity),
        out_shape=jax.ShapeDtypeStruct((rows, quarter), BF16),
        compiler_params=params(24),
        cost_estimate=cost(2 * slots * rows * quarter, 4 * slots * quarter),
    )(ids, own, back)


def halves_kernel(top_ref, bottom_ref, top_out, bottom_out):
    top_out[...] = top_ref[...]
    bottom_out[...] = bottom_ref[...]


def halves(first, second):
    rows, width = first.shape
    half = (rows // 2, width)
    shape = jax.ShapeDtypeStruct(half, BF16)
    return pl.pallas_call(
        halves_kernel,
        grid=(1,),
        in_specs=[
            pl.BlockSpec(half, lambda i: (0, 0)),
            pl.BlockSpec(half, lambda i: (1, 0)),
        ],
        out_specs=[whole(half)] * 2,
        out_shape=[shape, shape],
        compiler_params=params(24),
        cost_estimate=cost(rows, 4 * rows * width),
    )(first, second)


def held_kernel(*refs):
    del refs


def held(arrays, after):
    place = pl.BlockSpec(memory_space=pl.ANY)
    return pl.pallas_call(
        held_kernel,
        in_specs=[place] * (len(arrays) + len(after)),
        out_specs=[place] * len(arrays),
        out_shape=[jax.ShapeDtypeStruct(a.shape, a.dtype) for a in arrays],
        input_output_aliases={i: i for i in range(len(arrays))},
        compiler_params=params(24),
        cost_estimate=cost(1, 1),
    )(*arrays, *after)


def fixed(shape):
    return pl.BlockSpec(shape, lambda *_: (0,) * len(shape), pipeline_mode=pl.Buffered(1))


def accumulate(step, acc_ref, part):
    if isinstance(step, int):
        acc_ref[...] = part if step == 0 else acc_ref[...] + part
        return

    @pl.when(step == 0)
    def _():
        acc_ref[...] = part

    @pl.when(step > 0)
    def _():
        acc_ref[...] += part


def backward_early_kernel(order_ref, own, left, right, gate_ref, up_ref, down_ref, *refs):
    gate_acc, up_acc, back_acc, rows_ref = refs
    step = pl.program_id(0)
    for number, ref in enumerate((own, left, right)):

        @pl.when(step == number)
        def _():
            rows_ref[...] = ref[...]

    quarter = rows_ref.shape[1] // 2
    accumulate(step, back_acc, dot_nt(rows_ref[:, :quarter], down_ref[...]))
    accumulate(step, gate_acc, dot(rows_ref[:, quarter:], gate_ref[...]))
    accumulate(step, up_acc, dot(rows_ref[:, quarter:], up_ref[...]))


def backward_early(order, blocks, gate_mat, up_mat, down_mat):
    slots, pair = blocks[0].shape
    width, quarter = down_mat.shape[0], pair // 2
    weight = pl.BlockSpec((quarter, width), lambda i, order: (order[i], 0))
    return pl.pallas_call(
        backward_early_kernel,
        grid_spec=pltpu.PrefetchScalarGridSpec(
            num_scalar_prefetch=1,
            grid=(3,),
            in_specs=[fixed(b.shape) for b in blocks]
            + [weight, weight, pl.BlockSpec((width, quarter), lambda i, order: (0, order[i]))],
            out_specs=[whole((slots, width))] * 3,
            scratch_shapes=[pltpu.VMEM((slots, pair), BF16)],
        ),
        out_shape=[jax.ShapeDtypeStruct((slots, width), F32)] * 3,
        compiler_params=params(32),
        cost_estimate=lasting(30),
    )(order, *blocks, gate_mat, up_mat, down_mat)


def split(value, top_out, bottom_out):
    half = top_out.shape[0]
    top_out[...] = value[:half].astype(BF16)
    bottom_out[...] = value[half:].astype(BF16)


def backward_late_kernel(order_ref, top, bottom, gate_in, up_in, back_in, gate_ref, up_ref, down_ref, *refs):
    d_gate_ref, d_up_ref, top_out, bottom_out, rows_ref = refs
    half = top.shape[0]
    quarter = rows_ref.shape[1] // 2
    rows_ref[:half] = top[...]
    rows_ref[half:] = bottom[...]
    gate_pre = gate_in[...] + dot(rows_ref[:, quarter:], gate_ref[...])
    up_pre = up_in[...] + dot(rows_ref[:, quarter:], up_ref[...])
    back = back_in[...] + dot_nt(rows_ref[:, :quarter], down_ref[...])
    squash = jax.nn.sigmoid(gate_pre)
    turned = back * squash
    d_gate = (turned * up_pre * (1.0 + gate_pre * (1.0 - squash))).astype(BF16)
    d_up = (turned * gate_pre).astype(BF16)
    d_gate_ref[...] = d_gate
    d_up_ref[...] = d_up
    split(dot_nt(d_gate, gate_ref[...]) + dot_nt(d_up, up_ref[...]), top_out, bottom_out)


def backward_late(order, far, accs, gate_mat, up_mat, down_mat):
    half, pair = far[0].shape
    quarter = pair // 2
    slots, width = accs[0].shape
    rows = pl.BlockSpec((quarter, width), lambda i, order: (order[3], 0))
    columns = pl.BlockSpec((width, quarter), lambda i, order: (0, order[3]))
    wide = jax.ShapeDtypeStruct((slots, width), BF16)
    part = jax.ShapeDtypeStruct((half, quarter), BF16)
    return pl.pallas_call(
        backward_late_kernel,
        grid_spec=pltpu.PrefetchScalarGridSpec(
            num_scalar_prefetch=1,
            grid=(1,),
            in_specs=[fixed(b.shape) for b in (*far, *accs)] + [rows, rows, columns],
            out_specs=[whole(wide.shape)] * 2 + [whole(part.shape)] * 2,
            scratch_shapes=[pltpu.VMEM((slots, pair), BF16)],
        ),
        out_shape=[wide, wide, part, part],
        compiler_params=params(32),
        cost_estimate=cost(10 * slots * width * quarter, 6 * quarter * width),
    )(order, *far, *accs, gate_mat, up_mat, down_mat)


def forward_hidden_kernel(groups, order_ref, rows_hbm, gate_hbm, up_hbm, down_hbm, *refs):
    hidden_ref, top_out, bottom_out, rows, gates, ups, down, gate_acc, up_acc, sems = refs
    quarter = rows.shape[2]
    far = pl.multiple_of(order_ref[groups - 1] * quarter, 128)
    copies = []
    for i in range(groups):
        block = pl.ds(i * quarter, quarter)
        copies.append(
            [
                pltpu.make_async_copy(rows_hbm.at[:, block], rows.at[i], sems.at[0, i]),
                pltpu.make_async_copy(gate_hbm.at[block], gates.at[i], sems.at[1, i]),
                pltpu.make_async_copy(up_hbm.at[block], ups.at[i], sems.at[2, i]),
            ]
        )
    last = pltpu.make_async_copy(down_hbm.at[:, pl.ds(far, quarter)], down, sems.at[3, 0])
    for group in copies:
        for copy in group:
            copy.start()
    last.start()
    for i, group in enumerate(copies):
        for copy in group:
            copy.wait()
        accumulate(i, gate_acc, dot(rows[i], gates[i]))
        accumulate(i, up_acc, dot(rows[i], ups[i]))
    gate_pre = gate_acc[...]
    hidden = (gate_pre * jax.nn.sigmoid(gate_pre) * up_acc[...]).astype(BF16)
    hidden_ref[...] = hidden
    last.wait()
    split(dot(hidden, down[...]), top_out, bottom_out)


def forward_hidden(order, rows, gate_mat, up_mat, down_mat, groups):
    slots, quarter = rows.shape[0], rows.shape[1] // groups
    width = gate_mat.shape[1]
    wide = jax.ShapeDtypeStruct((slots, width), BF16)
    part = jax.ShapeDtypeStruct((slots // 2, quarter), BF16)
    return pl.pallas_call(
        functools.partial(forward_hidden_kernel, groups),
        grid_spec=pltpu.PrefetchScalarGridSpec(
            num_scalar_prefetch=1,
            grid=(1,),
            in_specs=[pl.BlockSpec(memory_space=pl.ANY)] * 4,
            out_specs=[whole(wide.shape)] + [whole(part.shape)] * 2,
            scratch_shapes=[
                pltpu.VMEM((groups, slots, quarter), BF16),
                pltpu.VMEM((groups, quarter, width), BF16),
                pltpu.VMEM((groups, quarter, width), BF16),
                pltpu.VMEM((width, quarter), BF16),
                pltpu.VMEM((slots, width), F32),
                pltpu.VMEM((slots, width), F32),
                pltpu.SemaphoreType.DMA((4, groups)),
            ],
        ),
        out_shape=[wide, part, part],
        compiler_params=params(60),
        cost_estimate=cost(18 * slots * width * quarter, 18 * quarter * width),
    )(order, rows, gate_mat, up_mat, down_mat)


def forward_rest_kernel(order_ref, hidden_ref, down_ref, top_ref, bottom_ref, left, right, own):
    step = pl.program_id(0)
    half = top_ref.shape[0]
    part = dot(hidden_ref[...], down_ref[...])

    @pl.when(step == 0)
    def _():
        left[:half] = (part[:half] + top_ref[...].astype(F32)).astype(BF16)
        left[half:] = part[half:].astype(BF16)

    @pl.when(step == 1)
    def _():
        right[:half] = part[:half].astype(BF16)
        right[half:] = (part[half:] + bottom_ref[...].astype(F32)).astype(BF16)

    @pl.when(step == 2)
    def _():
        own[...] = part.astype(BF16)


def forward_rest(order, hidden, down_mat, halves_in, hint):
    slots, width = hidden.shape
    half, quarter = halves_in[0].shape
    return pl.pallas_call(
        forward_rest_kernel,
        grid_spec=pltpu.PrefetchScalarGridSpec(
            num_scalar_prefetch=1,
            grid=(3,),
            in_specs=[
                whole((slots, width)),
                pl.BlockSpec((width, quarter), lambda i, order: (0, order[(i + 1) % 3])),
                whole((half, quarter)),
                whole((half, quarter)),
            ],
            out_specs=[whole((slots, quarter))] * 3,
        ),
        out_shape=[jax.ShapeDtypeStruct((slots, quarter), BF16)] * 3,
        compiler_params=params(32),
        cost_estimate=lasting(hint),
    )(order, hidden, down_mat, *halves_in)


def backward_rest_kernel(order_ref, d_gate_ref, d_up_ref, gate_ref, up_ref, *out_refs):
    step = pl.program_id(0)
    part = dot_nt(d_gate_ref[...], gate_ref[...]) + dot_nt(d_up_ref[...], up_ref[...])
    part = part.astype(BF16)
    for number, out_ref in enumerate(out_refs):

        @pl.when(step == number)
        def _():
            out_ref[...] = part


def backward_rest(order, d_gate, d_up, gate_mat, up_mat, quarter):
    slots, width = d_gate.shape
    weight = pl.BlockSpec((quarter, width), lambda i, order: (order[(i + 1) % 3], 0))
    return pl.pallas_call(
        backward_rest_kernel,
        grid_spec=pltpu.PrefetchScalarGridSpec(
            num_scalar_prefetch=1,
            grid=(3,),
            in_specs=[whole((slots, width)), whole((slots, width)), weight, weight],
            out_specs=[whole((slots, quarter))] * 3,
        ),
        out_shape=[jax.ShapeDtypeStruct((slots, quarter), BF16)] * 3,
        compiler_params=params(32),
        cost_estimate=cost(12 * slots * width * quarter, 6 * quarter * (2 * width + slots)),
    )(order, d_gate, d_up, gate_mat, up_mat)


def relay_add_kernel(left_ref, right_ref, top_ref, bottom_ref, left_out, right_out):
    half = top_ref.shape[0]
    left_out[:half] = (left_ref[:half].astype(F32) + top_ref[...].astype(F32)).astype(BF16)
    left_out[half:] = left_ref[half:]
    right_out[:half] = right_ref[:half]
    right_out[half:] = (right_ref[half:].astype(F32) + bottom_ref[...].astype(F32)).astype(BF16)


def relay_add(left, right, top, bottom):
    shape = jax.ShapeDtypeStruct(left.shape, BF16)
    return pl.pallas_call(
        relay_add_kernel,
        out_shape=[shape, shape],
        compiler_params=params(24),
        cost_estimate=lasting(1),
    )(left, right, top, bottom)


def sum_kernel(a_ref, b_ref, c_ref, *refs):
    total = a_ref[...].astype(F32) + b_ref[...].astype(F32) + c_ref[...].astype(F32)
    refs[-1][...] = total.astype(BF16)


def summed(a, b, c, hint, after=()):
    return pl.pallas_call(
        sum_kernel,
        grid=(1,),
        in_specs=[whole(a.shape)] * 3 + [pl.BlockSpec(memory_space=pl.ANY)] * len(after),
        out_specs=whole(a.shape),
        out_shape=jax.ShapeDtypeStruct(a.shape, BF16),
        compiler_params=params(24),
        cost_estimate=lasting(hint),
    )(a, b, c, *after)


def exchange(rows, experts):
    slots, width = rows.shape
    blocks = rows.reshape(experts, slots // experts, width)
    return lax.all_to_all(blocks, "expert", split_axis=0, concat_axis=0, tiled=True).reshape(
        slots, width
    )


def local(x_fwd, ids_fwd, gates_fwd, x_bwd, ids_bwd, gates_bwd, grad_in, w_gate, w_up, w_down):
    experts = lax.axis_size("expert")
    groups = lax.axis_size("dp")
    dp_rank = lax.axis_index("dp")
    rows_dev = x_fwd.shape[1]
    topk = ids_fwd.shape[2]
    capacity = rows_dev * topk * 3 // (2 * experts)
    quarter = x_fwd.shape[2] // groups
    order = (dp_rank + jnp.array([0, groups - 1, 1, 2], jnp.int32)) % groups
    gate_mat = w_gate[0, 0]
    up_mat = w_up[0, 0]
    down_mat = w_down[0, 0]
    fwd_ids, fwd_gates = ids_fwd[0].T, gates_fwd[0].T
    bwd_ids, bwd_gates = ids_bwd[0].T, gates_bwd[0].T

    bwd_rows = pack_pair(bwd_ids, bwd_gates, grad_in[0], x_bwd[0], experts, capacity)
    bwd_rows = exchange(bwd_rows, experts)
    fwd_rows = pack(fwd_ids, x_fwd[0], experts, capacity)
    (bwd_rows,) = held((bwd_rows,), (fwd_rows,))
    fwd_rows = exchange(fwd_rows, experts)

    left, right = shifted(bwd_rows, "dp", 1), shifted(bwd_rows, "dp", -1)
    top, bottom = halves(left, right)
    far = shifted(top, "dp", 1), shifted(bottom, "dp", -1)
    accs = backward_early(order, (bwd_rows, left, right), gate_mat, up_mat, down_mat)
    d_gate, d_up, top, bottom = backward_late(order, far, accs, gate_mat, up_mat, down_mat)
    bwd_far = shifted(top, "dp", -1), shifted(bottom, "dp", 1)
    bwd_left, bwd_right, bwd_own = backward_rest(order, d_gate, d_up, gate_mat, up_mat, quarter)
    bwd_left, bwd_right = relay_add(bwd_left, bwd_right, *bwd_far)
    bwd_left, bwd_right = shifted(bwd_left, "dp", -1), shifted(bwd_right, "dp", 1)

    hidden, top, bottom = forward_hidden(order, fwd_rows, gate_mat, up_mat, down_mat, groups)
    fwd_far = shifted(top, "dp", -1), shifted(bottom, "dp", 1)
    bwd_back = exchange(summed(bwd_own, bwd_left, bwd_right, 20, (top,)), experts)

    fwd_left, fwd_right, fwd_own = forward_rest(order, hidden, down_mat, fwd_far, 40)
    fwd_left, fwd_right = shifted(fwd_left, "dp", -1), shifted(fwd_right, "dp", 1)
    fwd_back = exchange(summed(fwd_own, fwd_left, fwd_right, 1), experts)

    layer_grad = combine(bwd_ids, grad_in[0], bwd_back, experts, capacity)
    sent_backward = shifted(layer_grad[None], "pipe", -1)
    layer_out = combine_gated(order, fwd_ids, fwd_gates, x_fwd[0], fwd_back, experts, capacity)
    sent_forward = shifted(layer_out[None], "pipe", 1)
    return (sent_forward, sent_backward)


def solution(mesh):
    in_specs = (
        P("pipe", "expert", None),
        P("pipe", "expert", None),
        P("pipe", "expert", None),
        P("pipe", "expert", None),
        P("pipe", "expert", None),
        P("pipe", "expert", None),
        P("pipe", "expert", "dp"),
        P("pipe", "expert", None, "dp"),
        P("pipe", "expert", None, "dp"),
        P("pipe", "expert", "dp", None),
    )
    out_specs = (P("pipe", "expert", "dp"), P("pipe", "expert", "dp"))
    return jax.shard_map(local, mesh=mesh, in_specs=in_specs, out_specs=out_specs, check_vma=False)
```

```python
import functools

import jax
import jax.numpy as jnp
from jax import lax
from jax.experimental import pallas as pl
from jax.experimental.pallas import tpu as pltpu
from jax.sharding import PartitionSpec as P

F32 = jnp.float32
BF16 = jnp.bfloat16
MIB = 1024 * 1024


def shifted(array, axis, by):
    count = lax.axis_size(axis)
    return lax.ppermute(array, axis, [(i, (i + by) % count) for i in range(count)])


def dot(a, b):
    return jnp.dot(a, b, preferred_element_type=F32)


def dot_nt(a, b):
    return lax.dot_general(a, b, (((1,), (1,)), ((), ())), preferred_element_type=F32)


def params(mib):
    return pltpu.CompilerParams(vmem_limit_bytes=mib * MIB)


def cost(flops, nbytes):
    return pl.CostEstimate(flops=int(flops), bytes_accessed=int(nbytes), transcendentals=0)


def lasting(microseconds):
    return pl.CostEstimate(flops=int(1e9 * microseconds), bytes_accessed=0, transcendentals=0)


def whole(shape):
    return pl.BlockSpec(shape, lambda *_: (0,) * len(shape))


def targets(ids, experts, capacity):
    topk, rows = ids.shape
    expert_of = lax.broadcasted_iota(jnp.int32, (experts, rows), 0)
    earlier = (
        lax.broadcasted_iota(jnp.int32, (rows, rows), 0)
        < lax.broadcasted_iota(jnp.int32, (rows, rows), 1)
    ).astype(BF16)
    before = jnp.zeros((experts, 1), F32)
    found = []
    for k in range(topk):
        named = (expert_of == ids[k : k + 1]).astype(F32)
        place = dot(named.astype(BF16), earlier) + before
        place = jnp.sum(named * place, axis=0, keepdims=True)
        found.append(ids[k : k + 1] * capacity + place.astype(jnp.int32))
        before = before + jnp.sum(named, axis=1, keepdims=True)
    return found


def as_column(row):
    rows = row.shape[1]
    same = lax.broadcasted_iota(jnp.int32, (rows, rows), 0) == lax.broadcasted_iota(
        jnp.int32, (rows, rows), 1
    )
    return jnp.sum(jnp.where(same, row, jnp.zeros_like(row)), axis=1, keepdims=True)


def slot_hits(ids, experts, capacity):
    rows = ids.shape[1]
    slot = lax.broadcasted_iota(jnp.int32, (experts * capacity, rows), 0)
    return [slot == t for t in targets(ids, experts, capacity)]


def one_hot(hit):
    return jnp.where(hit, 1.0, 0.0).astype(BF16)


def pack_kernel(experts, capacity, ids_ref, source_ref, out_ref):
    hits = slot_hits(ids_ref[...], experts, capacity)
    chosen = one_hot(functools.reduce(jnp.logical_or, hits))
    out_ref[...] = dot(chosen, source_ref[...]).astype(BF16)


def pack(ids, source, experts, capacity):
    slots, width = experts * capacity, source.shape[1]
    return pl.pallas_call(
        functools.partial(pack_kernel, experts, capacity),
        out_shape=jax.ShapeDtypeStruct((slots, width), BF16),
        compiler_params=params(32),
        cost_estimate=cost(2 * slots * source.size, 4 * slots * width),
    )(ids, source)


def pack_pair_kernel(experts, capacity, ids_ref, gates_ref, grad_ref, source_hbm, out_ref, source, sem):
    quarter = grad_ref.shape[1]
    start = pl.multiple_of(lax.axis_index("dp") * quarter, 128)
    copy = pltpu.make_async_copy(source_hbm.at[:, pl.ds(start, quarter)], source, sem)
    copy.start()
    hits = slot_hits(ids_ref[...], experts, capacity)
    chosen = one_hot(functools.reduce(jnp.logical_or, hits))
    gate = sum(
        jnp.sum(jnp.where(hit, gates_ref[k : k + 1], 0.0), axis=1, keepdims=True)
        for k, hit in enumerate(hits)
    )
    out_ref[:, :quarter] = (gate * dot(chosen, grad_ref[...])).astype(BF16)
    copy.wait()
    out_ref[:, quarter:] = dot(chosen, source[...]).astype(BF16)


def pack_pair(ids, gates, grad, source, experts, capacity):
    rows, quarter = grad.shape
    slots = experts * capacity
    return pl.pallas_call(
        functools.partial(pack_pair_kernel, experts, capacity),
        grid=(1,),
        in_specs=[
            whole(ids.shape),
            whole(gates.shape),
            whole(grad.shape),
            pl.BlockSpec(memory_space=pl.ANY),
        ],
        out_specs=whole((slots, 2 * quarter)),
        out_shape=jax.ShapeDtypeStruct((slots, 2 * quarter), BF16),
        scratch_shapes=[pltpu.VMEM((rows, quarter), BF16), pltpu.SemaphoreType.DMA],
        compiler_params=params(60),
        cost_estimate=cost(4 * slots * rows * quarter, 8 * slots * quarter),
    )(ids, gates, grad, source)


def token_hits(ids, experts, capacity):
    rows = ids.shape[1]
    slot = lax.broadcasted_iota(jnp.int32, (rows, experts * capacity), 1)
    return [slot == as_column(t) for t in targets(ids, experts, capacity)]


def combine_gated_kernel(experts, capacity, rank_ref, ids_ref, gates_ref, own_ref, back_ref, out_ref):
    total = own_ref[...].astype(F32)
    for k, hit in enumerate(token_hits(ids_ref[...], experts, capacity)):
        total += as_column(gates_ref[k : k + 1]) * dot(one_hot(hit), back_ref[...])
    out_ref[...] = total.astype(BF16)


def combine_kernel(experts, capacity, ids_ref, own_ref, back_ref, out_ref):
    hits = token_hits(ids_ref[...], experts, capacity)
    chosen = one_hot(functools.reduce(jnp.logical_or, hits))
    total = own_ref[...].astype(F32) + dot(chosen, back_ref[...])
    out_ref[...] = total.astype(BF16)


def combine_gated(rank, ids, gates, own, back, experts, capacity):
    rows = ids.shape[1]
    slots, quarter = back.shape
    return pl.pallas_call(
        functools.partial(combine_gated_kernel, experts, capacity),
        grid_spec=pltpu.PrefetchScalarGridSpec(
            num_scalar_prefetch=1,
            grid=(1,),
            in_specs=[
                whole(ids.shape),
                whole(gates.shape),
                pl.BlockSpec((rows, quarter), lambda i, order: (0, order[0])),
                whole(back.shape),
            ],
            out_specs=whole((rows, quarter)),
        ),
        out_shape=jax.ShapeDtypeStruct((rows, quarter), BF16),
        compiler_params=params(24),
        cost_estimate=cost(4 * slots * rows * quarter, 4 * slots * quarter),
    )(rank, ids, gates, own, back)


def combine(ids, own, back, experts, capacity):
    rows = ids.shape[1]
    slots, quarter = back.shape
    return pl.pallas_call(
        functools.partial(combine_kernel, experts, capacity),
        out_shape=jax.ShapeDtypeStruct((rows, quarter), BF16),
        compiler_params=params(24),
        cost_estimate=cost(2 * slots * rows * quarter, 4 * slots * quarter),
    )(ids, own, back)


def halves_kernel(top_ref, bottom_ref, top_out, bottom_out):
    top_out[...] = top_ref[...]
    bottom_out[...] = bottom_ref[...]


def halves(first, second):
    rows, width = first.shape
    half = (rows // 2, width)
    shape = jax.ShapeDtypeStruct(half, BF16)
    return pl.pallas_call(
        halves_kernel,
        grid=(1,),
        in_specs=[
            pl.BlockSpec(half, lambda i: (0, 0)),
            pl.BlockSpec(half, lambda i: (1, 0)),
        ],
        out_specs=[whole(half)] * 2,
        out_shape=[shape, shape],
        compiler_params=params(24),
        cost_estimate=cost(rows, 4 * rows * width),
    )(first, second)


def held_kernel(*refs):
    del refs


def held(arrays, after):
    place = pl.BlockSpec(memory_space=pl.ANY)
    return pl.pallas_call(
        held_kernel,
        in_specs=[place] * (len(arrays) + len(after)),
        out_specs=[place] * len(arrays),
        out_shape=[jax.ShapeDtypeStruct(a.shape, a.dtype) for a in arrays],
        input_output_aliases={i: i for i in range(len(arrays))},
        compiler_params=params(24),
        cost_estimate=cost(1, 1),
    )(*arrays, *after)


def fixed(shape):
    return pl.BlockSpec(shape, lambda *_: (0,) * len(shape), pipeline_mode=pl.Buffered(1))


def accumulate(step, acc_ref, part):
    if isinstance(step, int):
        acc_ref[...] = part if step == 0 else acc_ref[...] + part
        return

    @pl.when(step == 0)
    def _():
        acc_ref[...] = part

    @pl.when(step > 0)
    def _():
        acc_ref[...] += part


def backward_early_kernel(order_ref, own, left, right, gate_ref, up_ref, down_ref, *refs):
    gate_acc, up_acc, back_acc, rows_ref = refs
    step = pl.program_id(0)
    for number, ref in enumerate((own, left, right)):

        @pl.when(step == number)
        def _():
            rows_ref[...] = ref[...]

    quarter = rows_ref.shape[1] // 2
    accumulate(step, back_acc, dot_nt(rows_ref[:, :quarter], down_ref[...]))
    accumulate(step, gate_acc, dot(rows_ref[:, quarter:], gate_ref[...]))
    accumulate(step, up_acc, dot(rows_ref[:, quarter:], up_ref[...]))


def backward_early(order, blocks, gate_mat, up_mat, down_mat):
    slots, pair = blocks[0].shape
    width, quarter = down_mat.shape[0], pair // 2
    weight = pl.BlockSpec((quarter, width), lambda i, order: (order[i], 0))
    return pl.pallas_call(
        backward_early_kernel,
        grid_spec=pltpu.PrefetchScalarGridSpec(
            num_scalar_prefetch=1,
            grid=(3,),
            in_specs=[fixed(b.shape) for b in blocks]
            + [weight, weight, pl.BlockSpec((width, quarter), lambda i, order: (0, order[i]))],
            out_specs=[whole((slots, width))] * 3,
            scratch_shapes=[pltpu.VMEM((slots, pair), BF16)],
        ),
        out_shape=[jax.ShapeDtypeStruct((slots, width), F32)] * 3,
        compiler_params=params(32),
        cost_estimate=lasting(30),
    )(order, *blocks, gate_mat, up_mat, down_mat)


def split(value, top_out, bottom_out):
    half = top_out.shape[0]
    top_out[...] = value[:half].astype(BF16)
    bottom_out[...] = value[half:].astype(BF16)


def backward_late_kernel(order_ref, top, bottom, gate_in, up_in, back_in, gate_ref, up_ref, down_ref, *refs):
    d_gate_ref, d_up_ref, top_out, bottom_out, rows_ref = refs
    half = top.shape[0]
    quarter = rows_ref.shape[1] // 2
    rows_ref[:half] = top[...]
    rows_ref[half:] = bottom[...]
    gate_pre = gate_in[...] + dot(rows_ref[:, quarter:], gate_ref[...])
    up_pre = up_in[...] + dot(rows_ref[:, quarter:], up_ref[...])
    back = back_in[...] + dot_nt(rows_ref[:, :quarter], down_ref[...])
    squash = jax.nn.sigmoid(gate_pre)
    turned = back * squash
    d_gate = (turned * up_pre * (1.0 + gate_pre * (1.0 - squash))).astype(BF16)
    d_up = (turned * gate_pre).astype(BF16)
    d_gate_ref[...] = d_gate
    d_up_ref[...] = d_up
    split(dot_nt(d_gate, gate_ref[...]) + dot_nt(d_up, up_ref[...]), top_out, bottom_out)


def backward_late(order, far, accs, gate_mat, up_mat, down_mat):
    half, pair = far[0].shape
    quarter = pair // 2
    slots, width = accs[0].shape
    rows = pl.BlockSpec((quarter, width), lambda i, order: (order[3], 0))
    columns = pl.BlockSpec((width, quarter), lambda i, order: (0, order[3]))
    wide = jax.ShapeDtypeStruct((slots, width), BF16)
    part = jax.ShapeDtypeStruct((half, quarter), BF16)
    return pl.pallas_call(
        backward_late_kernel,
        grid_spec=pltpu.PrefetchScalarGridSpec(
            num_scalar_prefetch=1,
            grid=(1,),
            in_specs=[fixed(b.shape) for b in (*far, *accs)] + [rows, rows, columns],
            out_specs=[whole(wide.shape)] * 2 + [whole(part.shape)] * 2,
            scratch_shapes=[pltpu.VMEM((slots, pair), BF16)],
        ),
        out_shape=[wide, wide, part, part],
        compiler_params=params(32),
        cost_estimate=cost(10 * slots * width * quarter, 6 * quarter * width),
    )(order, *far, *accs, gate_mat, up_mat, down_mat)


def forward_hidden_kernel(groups, order_ref, rows_hbm, gate_hbm, up_hbm, down_hbm, *refs):
    hidden_ref, top_out, bottom_out, rows, gates, ups, down, gate_acc, up_acc, sems = refs
    quarter = rows.shape[2]
    far = pl.multiple_of(order_ref[groups - 1] * quarter, 128)
    copies = []
    for i in range(groups):
        block = pl.ds(i * quarter, quarter)
        copies.append(
            [
                pltpu.make_async_copy(rows_hbm.at[:, block], rows.at[i], sems.at[0, i]),
                pltpu.make_async_copy(gate_hbm.at[block], gates.at[i], sems.at[1, i]),
                pltpu.make_async_copy(up_hbm.at[block], ups.at[i], sems.at[2, i]),
            ]
        )
    last = pltpu.make_async_copy(down_hbm.at[:, pl.ds(far, quarter)], down, sems.at[3, 0])
    for group in copies:
        for copy in group:
            copy.start()
    last.start()
    for i, group in enumerate(copies):
        for copy in group:
            copy.wait()
        accumulate(i, gate_acc, dot(rows[i], gates[i]))
        accumulate(i, up_acc, dot(rows[i], ups[i]))
    gate_pre = gate_acc[...]
    hidden = (gate_pre * jax.nn.sigmoid(gate_pre) * up_acc[...]).astype(BF16)
    hidden_ref[...] = hidden
    last.wait()
    split(dot(hidden, down[...]), top_out, bottom_out)


def forward_hidden(order, rows, gate_mat, up_mat, down_mat, groups):
    slots, quarter = rows.shape[0], rows.shape[1] // groups
    width = gate_mat.shape[1]
    wide = jax.ShapeDtypeStruct((slots, width), BF16)
    part = jax.ShapeDtypeStruct((slots // 2, quarter), BF16)
    return pl.pallas_call(
        functools.partial(forward_hidden_kernel, groups),
        grid_spec=pltpu.PrefetchScalarGridSpec(
            num_scalar_prefetch=1,
            grid=(1,),
            in_specs=[pl.BlockSpec(memory_space=pl.ANY)] * 4,
            out_specs=[whole(wide.shape)] + [whole(part.shape)] * 2,
            scratch_shapes=[
                pltpu.VMEM((groups, slots, quarter), BF16),
                pltpu.VMEM((groups, quarter, width), BF16),
                pltpu.VMEM((groups, quarter, width), BF16),
                pltpu.VMEM((width, quarter), BF16),
                pltpu.VMEM((slots, width), F32),
                pltpu.VMEM((slots, width), F32),
                pltpu.SemaphoreType.DMA((4, groups)),
            ],
        ),
        out_shape=[wide, part, part],
        compiler_params=params(60),
        cost_estimate=cost(18 * slots * width * quarter, 18 * quarter * width),
    )(order, rows, gate_mat, up_mat, down_mat)


def forward_rest_kernel(order_ref, hidden_ref, down_ref, top_ref, bottom_ref, left, right):
    step = pl.program_id(0)
    half = top_ref.shape[0]
    part = dot(hidden_ref[...], down_ref[...])

    @pl.when(step == 0)
    def _():
        left[:half] = (part[:half] + top_ref[...].astype(F32)).astype(BF16)
        left[half:] = part[half:].astype(BF16)

    @pl.when(step == 1)
    def _():
        right[:half] = part[:half].astype(BF16)
        right[half:] = (part[half:] + bottom_ref[...].astype(F32)).astype(BF16)


def forward_rest(order, hidden, down_mat, halves_in, hint):
    slots, width = hidden.shape
    half, quarter = halves_in[0].shape
    return pl.pallas_call(
        forward_rest_kernel,
        grid_spec=pltpu.PrefetchScalarGridSpec(
            num_scalar_prefetch=1,
            grid=(2,),
            in_specs=[
                whole((slots, width)),
                pl.BlockSpec((width, quarter), lambda i, order: (0, order[i + 1])),
                whole((half, quarter)),
                whole((half, quarter)),
            ],
            out_specs=[whole((slots, quarter))] * 2,
        ),
        out_shape=[jax.ShapeDtypeStruct((slots, quarter), BF16)] * 2,
        compiler_params=params(60),
        cost_estimate=lasting(hint),
    )(order, hidden, down_mat, *halves_in)


def forward_own_kernel(order_ref, hidden_ref, down_ref, out_ref):
    out_ref[...] = dot(hidden_ref[...], down_ref[...]).astype(BF16)


def forward_own(order, hidden, down_mat, quarter):
    slots, width = hidden.shape
    return pl.pallas_call(
        forward_own_kernel,
        grid_spec=pltpu.PrefetchScalarGridSpec(
            num_scalar_prefetch=1,
            grid=(1,),
            in_specs=[
                whole((slots, width)),
                pl.BlockSpec((width, quarter), lambda i, order: (0, order[0])),
            ],
            out_specs=whole((slots, quarter)),
        ),
        out_shape=jax.ShapeDtypeStruct((slots, quarter), BF16),
        compiler_params=params(32),
        cost_estimate=cost(2 * slots * width * quarter, 2 * quarter * (width + slots)),
    )(order, hidden, down_mat)


def backward_rest_kernel(order_ref, d_gate_ref, d_up_ref, gate_ref, up_ref, *out_refs):
    step = pl.program_id(0)
    part = dot_nt(d_gate_ref[...], gate_ref[...]) + dot_nt(d_up_ref[...], up_ref[...])
    part = part.astype(BF16)
    for number, out_ref in enumerate(out_refs):

        @pl.when(step == number)
        def _():
            out_ref[...] = part


def backward_rest(order, d_gate, d_up, gate_mat, up_mat, quarter):
    slots, width = d_gate.shape
    weight = pl.BlockSpec((quarter, width), lambda i, order: (order[(i + 1) % 3], 0))
    return pl.pallas_call(
        backward_rest_kernel,
        grid_spec=pltpu.PrefetchScalarGridSpec(
            num_scalar_prefetch=1,
            grid=(3,),
            in_specs=[whole((slots, width)), whole((slots, width)), weight, weight],
            out_specs=[whole((slots, quarter))] * 3,
        ),
        out_shape=[jax.ShapeDtypeStruct((slots, quarter), BF16)] * 3,
        compiler_params=params(32),
        cost_estimate=cost(12 * slots * width * quarter, 6 * quarter * (2 * width + slots)),
    )(order, d_gate, d_up, gate_mat, up_mat)


def relay_add_kernel(left_ref, right_ref, top_ref, bottom_ref, left_out, right_out):
    half = top_ref.shape[0]
    left_out[:half] = (left_ref[:half].astype(F32) + top_ref[...].astype(F32)).astype(BF16)
    left_out[half:] = left_ref[half:]
    right_out[:half] = right_ref[:half]
    right_out[half:] = (right_ref[half:].astype(F32) + bottom_ref[...].astype(F32)).astype(BF16)


def relay_add(left, right, top, bottom):
    shape = jax.ShapeDtypeStruct(left.shape, BF16)
    return pl.pallas_call(
        relay_add_kernel,
        out_shape=[shape, shape],
        compiler_params=params(24),
        cost_estimate=lasting(1),
    )(left, right, top, bottom)


def sum_kernel(a_ref, b_ref, c_ref, *refs):
    total = a_ref[...].astype(F32) + b_ref[...].astype(F32) + c_ref[...].astype(F32)
    refs[-1][...] = total.astype(BF16)


def summed(a, b, c, hint, after=()):
    return pl.pallas_call(
        sum_kernel,
        grid=(1,),
        in_specs=[whole(a.shape)] * 3 + [pl.BlockSpec(memory_space=pl.ANY)] * len(after),
        out_specs=whole(a.shape),
        out_shape=jax.ShapeDtypeStruct(a.shape, BF16),
        compiler_params=params(24),
        cost_estimate=lasting(hint),
    )(a, b, c, *after)


def exchange(rows, experts):
    slots, width = rows.shape
    blocks = rows.reshape(experts, slots // experts, width)
    return lax.all_to_all(blocks, "expert", split_axis=0, concat_axis=0, tiled=True).reshape(
        slots, width
    )


def local(x_fwd, ids_fwd, gates_fwd, x_bwd, ids_bwd, gates_bwd, grad_in, w_gate, w_up, w_down):
    experts = lax.axis_size("expert")
    groups = lax.axis_size("dp")
    dp_rank = lax.axis_index("dp")
    rows_dev = x_fwd.shape[1]
    topk = ids_fwd.shape[2]
    capacity = rows_dev * topk * 3 // (2 * experts)
    quarter = x_fwd.shape[2] // groups
    order = (dp_rank + jnp.array([0, groups - 1, 1, 2], jnp.int32)) % groups
    gate_mat = w_gate[0, 0]
    up_mat = w_up[0, 0]
    down_mat = w_down[0, 0]
    fwd_ids, fwd_gates = ids_fwd[0].T, gates_fwd[0].T
    bwd_ids, bwd_gates = ids_bwd[0].T, gates_bwd[0].T

    bwd_rows = pack_pair(bwd_ids, bwd_gates, grad_in[0], x_bwd[0], experts, capacity)
    bwd_rows = exchange(bwd_rows, experts)
    fwd_rows = pack(fwd_ids, x_fwd[0], experts, capacity)
    (bwd_rows,) = held((bwd_rows,), (fwd_rows,))
    fwd_rows = exchange(fwd_rows, experts)

    left, right = shifted(bwd_rows, "dp", 1), shifted(bwd_rows, "dp", -1)
    top, bottom = halves(left, right)
    far = shifted(top, "dp", 1), shifted(bottom, "dp", -1)
    accs = backward_early(order, (bwd_rows, left, right), gate_mat, up_mat, down_mat)
    d_gate, d_up, top, bottom = backward_late(order, far, accs, gate_mat, up_mat, down_mat)
    bwd_far = shifted(top, "dp", -1), shifted(bottom, "dp", 1)
    bwd_left, bwd_right, bwd_own = backward_rest(order, d_gate, d_up, gate_mat, up_mat, quarter)
    bwd_left, bwd_right = relay_add(bwd_left, bwd_right, *bwd_far)
    bwd_left, bwd_right = shifted(bwd_left, "dp", -1), shifted(bwd_right, "dp", 1)

    hidden, top, bottom = forward_hidden(order, fwd_rows, gate_mat, up_mat, down_mat, groups)
    fwd_far = shifted(top, "dp", -1), shifted(bottom, "dp", 1)
    bwd_back = exchange(summed(bwd_own, bwd_left, bwd_right, 20, (top,)), experts)

    fwd_left, fwd_right = forward_rest(order, hidden, down_mat, fwd_far, 40)
    fwd_own = forward_own(order, hidden, down_mat, quarter)
    fwd_left, fwd_right = shifted(fwd_left, "dp", -1), shifted(fwd_right, "dp", 1)
    fwd_back = exchange(summed(fwd_own, fwd_left, fwd_right, 1), experts)

    layer_grad = combine(bwd_ids, grad_in[0], bwd_back, experts, capacity)
    sent_backward = shifted(layer_grad[None], "pipe", -1)
    layer_out = combine_gated(order, fwd_ids, fwd_gates, x_fwd[0], fwd_back, experts, capacity)
    sent_forward = shifted(layer_out[None], "pipe", 1)
    return (sent_forward, sent_backward)


def solution(mesh):
    in_specs = (
        P("pipe", "expert", None),
        P("pipe", "expert", None),
        P("pipe", "expert", None),
        P("pipe", "expert", None),
        P("pipe", "expert", None),
        P("pipe", "expert", None),
        P("pipe", "expert", "dp"),
        P("pipe", "expert", None, "dp"),
        P("pipe", "expert", None, "dp"),
        P("pipe", "expert", "dp", None),
    )
    out_specs = (P("pipe", "expert", "dp"), P("pipe", "expert", "dp"))
    return jax.shard_map(local, mesh=mesh, in_specs=in_specs, out_specs=out_specs, check_vma=False)
```

```python
import functools

import jax
import jax.numpy as jnp
from jax import lax
from jax.experimental import pallas as pl
from jax.experimental.pallas import tpu as pltpu
from jax.sharding import PartitionSpec as P

F32 = jnp.float32
BF16 = jnp.bfloat16
MIB = 1024 * 1024


def shifted(array, axis, by):
    count = lax.axis_size(axis)
    return lax.ppermute(array, axis, [(i, (i + by) % count) for i in range(count)])


def dot(a, b):
    return jnp.dot(a, b, preferred_element_type=F32)


def dot_nt(a, b):
    return lax.dot_general(a, b, (((1,), (1,)), ((), ())), preferred_element_type=F32)


def params(mib):
    return pltpu.CompilerParams(vmem_limit_bytes=mib * MIB)


def cost(flops, nbytes):
    return pl.CostEstimate(flops=int(flops), bytes_accessed=int(nbytes), transcendentals=0)


def lasting(microseconds):
    return pl.CostEstimate(flops=int(1e9 * microseconds), bytes_accessed=0, transcendentals=0)


def whole(shape):
    return pl.BlockSpec(shape, lambda *_: (0,) * len(shape))


def targets(ids, experts, capacity):
    topk, rows = ids.shape
    expert_of = lax.broadcasted_iota(jnp.int32, (experts, rows), 0)
    earlier = (
        lax.broadcasted_iota(jnp.int32, (rows, rows), 0)
        < lax.broadcasted_iota(jnp.int32, (rows, rows), 1)
    ).astype(BF16)
    before = jnp.zeros((experts, 1), F32)
    found = []
    for k in range(topk):
        named = (expert_of == ids[k : k + 1]).astype(F32)
        place = dot(named.astype(BF16), earlier) + before
        place = jnp.sum(named * place, axis=0, keepdims=True)
        found.append(ids[k : k + 1] * capacity + place.astype(jnp.int32))
        before = before + jnp.sum(named, axis=1, keepdims=True)
    return found


def as_column(row):
    rows = row.shape[1]
    same = lax.broadcasted_iota(jnp.int32, (rows, rows), 0) == lax.broadcasted_iota(
        jnp.int32, (rows, rows), 1
    )
    return jnp.sum(jnp.where(same, row, jnp.zeros_like(row)), axis=1, keepdims=True)


def slot_hits(ids, experts, capacity):
    rows = ids.shape[1]
    slot = lax.broadcasted_iota(jnp.int32, (experts * capacity, rows), 0)
    return [slot == t for t in targets(ids, experts, capacity)]


def one_hot(hit):
    return jnp.where(hit, 1.0, 0.0).astype(BF16)


def pack_kernel(experts, capacity, ids_ref, source_ref, out_ref):
    hits = slot_hits(ids_ref[...], experts, capacity)
    chosen = one_hot(functools.reduce(jnp.logical_or, hits))
    out_ref[...] = dot(chosen, source_ref[...]).astype(BF16)


def pack(ids, source, experts, capacity):
    slots, width = experts * capacity, source.shape[1]
    return pl.pallas_call(
        functools.partial(pack_kernel, experts, capacity),
        out_shape=jax.ShapeDtypeStruct((slots, width), BF16),
        compiler_params=params(32),
        cost_estimate=cost(2 * slots * source.size, 4 * slots * width),
    )(ids, source)


def pack_pair_kernel(experts, capacity, ids_ref, gates_ref, grad_ref, source_hbm, out_ref, source, sem):
    quarter = grad_ref.shape[1]
    start = pl.multiple_of(lax.axis_index("dp") * quarter, 128)
    copy = pltpu.make_async_copy(source_hbm.at[:, pl.ds(start, quarter)], source, sem)
    copy.start()
    hits = slot_hits(ids_ref[...], experts, capacity)
    chosen = one_hot(functools.reduce(jnp.logical_or, hits))
    gate = sum(
        jnp.sum(jnp.where(hit, gates_ref[k : k + 1], 0.0), axis=1, keepdims=True)
        for k, hit in enumerate(hits)
    )
    out_ref[:, :quarter] = (gate * dot(chosen, grad_ref[...])).astype(BF16)
    copy.wait()
    out_ref[:, quarter:] = dot(chosen, source[...]).astype(BF16)


def pack_pair(ids, gates, grad, source, experts, capacity):
    rows, quarter = grad.shape
    slots = experts * capacity
    return pl.pallas_call(
        functools.partial(pack_pair_kernel, experts, capacity),
        grid=(1,),
        in_specs=[
            whole(ids.shape),
            whole(gates.shape),
            whole(grad.shape),
            pl.BlockSpec(memory_space=pl.ANY),
        ],
        out_specs=whole((slots, 2 * quarter)),
        out_shape=jax.ShapeDtypeStruct((slots, 2 * quarter), BF16),
        scratch_shapes=[pltpu.VMEM((rows, quarter), BF16), pltpu.SemaphoreType.DMA],
        compiler_params=params(60),
        cost_estimate=cost(4 * slots * rows * quarter, 8 * slots * quarter),
    )(ids, gates, grad, source)


def token_hits(ids, experts, capacity):
    rows = ids.shape[1]
    slot = lax.broadcasted_iota(jnp.int32, (rows, experts * capacity), 1)
    return [slot == as_column(t) for t in targets(ids, experts, capacity)]


def combine_gated_kernel(experts, capacity, rank_ref, ids_ref, gates_ref, own_ref, back_ref, out_ref):
    total = own_ref[...].astype(F32)
    for k, hit in enumerate(token_hits(ids_ref[...], experts, capacity)):
        total += as_column(gates_ref[k : k + 1]) * dot(one_hot(hit), back_ref[...])
    out_ref[...] = total.astype(BF16)


def combine_kernel(experts, capacity, ids_ref, own_ref, back_ref, out_ref):
    hits = token_hits(ids_ref[...], experts, capacity)
    chosen = one_hot(functools.reduce(jnp.logical_or, hits))
    total = own_ref[...].astype(F32) + dot(chosen, back_ref[...])
    out_ref[...] = total.astype(BF16)


def combine_gated(rank, ids, gates, own, back, experts, capacity):
    rows = ids.shape[1]
    slots, quarter = back.shape
    return pl.pallas_call(
        functools.partial(combine_gated_kernel, experts, capacity),
        grid_spec=pltpu.PrefetchScalarGridSpec(
            num_scalar_prefetch=1,
            grid=(1,),
            in_specs=[
                whole(ids.shape),
                whole(gates.shape),
                pl.BlockSpec((rows, quarter), lambda i, order: (0, order[0])),
                whole(back.shape),
            ],
            out_specs=whole((rows, quarter)),
        ),
        out_shape=jax.ShapeDtypeStruct((rows, quarter), BF16),
        compiler_params=params(24),
        cost_estimate=cost(4 * slots * rows * quarter, 4 * slots * quarter),
    )(rank, ids, gates, own, back)


def combine(ids, own, back, experts, capacity):
    rows = ids.shape[1]
    slots, quarter = back.shape
    return pl.pallas_call(
        functools.partial(combine_kernel, experts, capacity),
        out_shape=jax.ShapeDtypeStruct((rows, quarter), BF16),
        compiler_params=params(24),
        cost_estimate=cost(2 * slots * rows * quarter, 4 * slots * quarter),
    )(ids, own, back)


def halves_kernel(top_ref, bottom_ref, top_out, bottom_out):
    top_out[...] = top_ref[...]
    bottom_out[...] = bottom_ref[...]


def halves(first, second):
    rows, width = first.shape
    half = (rows // 2, width)
    shape = jax.ShapeDtypeStruct(half, BF16)
    return pl.pallas_call(
        halves_kernel,
        grid=(1,),
        in_specs=[
            pl.BlockSpec(half, lambda i: (0, 0)),
            pl.BlockSpec(half, lambda i: (1, 0)),
        ],
        out_specs=[whole(half)] * 2,
        out_shape=[shape, shape],
        compiler_params=params(24),
        cost_estimate=cost(rows, 4 * rows * width),
    )(first, second)


def held_kernel(*refs):
    del refs


def held(arrays, after):
    place = pl.BlockSpec(memory_space=pl.ANY)
    return pl.pallas_call(
        held_kernel,
        in_specs=[place] * (len(arrays) + len(after)),
        out_specs=[place] * len(arrays),
        out_shape=[jax.ShapeDtypeStruct(a.shape, a.dtype) for a in arrays],
        input_output_aliases={i: i for i in range(len(arrays))},
        compiler_params=params(24),
        cost_estimate=cost(1, 1),
    )(*arrays, *after)


def fixed(shape):
    return pl.BlockSpec(shape, lambda *_: (0,) * len(shape), pipeline_mode=pl.Buffered(1))


def accumulate(step, acc_ref, part):
    if isinstance(step, int):
        acc_ref[...] = part if step == 0 else acc_ref[...] + part
        return

    @pl.when(step == 0)
    def _():
        acc_ref[...] = part

    @pl.when(step > 0)
    def _():
        acc_ref[...] += part


def backward_early_kernel(order_ref, own, left, right, gate_ref, up_ref, down_ref, *refs):
    gate_acc, up_acc, back_acc, rows_ref = refs
    step = pl.program_id(0)
    for number, ref in enumerate((own, left, right)):

        @pl.when(step == number)
        def _():
            rows_ref[...] = ref[...]

    quarter = rows_ref.shape[1] // 2
    accumulate(step, back_acc, dot_nt(rows_ref[:, :quarter], down_ref[...]))
    accumulate(step, gate_acc, dot(rows_ref[:, quarter:], gate_ref[...]))
    accumulate(step, up_acc, dot(rows_ref[:, quarter:], up_ref[...]))


def backward_early(order, blocks, gate_mat, up_mat, down_mat):
    slots, pair = blocks[0].shape
    width, quarter = down_mat.shape[0], pair // 2
    weight = pl.BlockSpec((quarter, width), lambda i, order: (order[i], 0))
    return pl.pallas_call(
        backward_early_kernel,
        grid_spec=pltpu.PrefetchScalarGridSpec(
            num_scalar_prefetch=1,
            grid=(3,),
            in_specs=[fixed(b.shape) for b in blocks]
            + [weight, weight, pl.BlockSpec((width, quarter), lambda i, order: (0, order[i]))],
            out_specs=[whole((slots, width))] * 3,
            scratch_shapes=[pltpu.VMEM((slots, pair), BF16)],
        ),
        out_shape=[jax.ShapeDtypeStruct((slots, width), F32)] * 3,
        compiler_params=params(32),
        cost_estimate=lasting(30),
    )(order, *blocks, gate_mat, up_mat, down_mat)


def split(value, top_out, bottom_out):
    half = top_out.shape[0]
    top_out[...] = value[:half].astype(BF16)
    bottom_out[...] = value[half:].astype(BF16)


def backward_late_kernel(order_ref, top, bottom, gate_in, up_in, back_in, gate_ref, up_ref, down_ref, *refs):
    d_gate_ref, d_up_ref, top_out, bottom_out, rows_ref = refs
    half = top.shape[0]
    quarter = rows_ref.shape[1] // 2
    rows_ref[:half] = top[...]
    rows_ref[half:] = bottom[...]
    gate_pre = gate_in[...] + dot(rows_ref[:, quarter:], gate_ref[...])
    up_pre = up_in[...] + dot(rows_ref[:, quarter:], up_ref[...])
    back = back_in[...] + dot_nt(rows_ref[:, :quarter], down_ref[...])
    squash = jax.nn.sigmoid(gate_pre)
    turned = back * squash
    d_gate = (turned * up_pre * (1.0 + gate_pre * (1.0 - squash))).astype(BF16)
    d_up = (turned * gate_pre).astype(BF16)
    d_gate_ref[...] = d_gate
    d_up_ref[...] = d_up
    split(dot_nt(d_gate, gate_ref[...]) + dot_nt(d_up, up_ref[...]), top_out, bottom_out)


def backward_late(order, far, accs, gate_mat, up_mat, down_mat):
    half, pair = far[0].shape
    quarter = pair // 2
    slots, width = accs[0].shape
    rows = pl.BlockSpec((quarter, width), lambda i, order: (order[3], 0))
    columns = pl.BlockSpec((width, quarter), lambda i, order: (0, order[3]))
    wide = jax.ShapeDtypeStruct((slots, width), BF16)
    part = jax.ShapeDtypeStruct((half, quarter), BF16)
    return pl.pallas_call(
        backward_late_kernel,
        grid_spec=pltpu.PrefetchScalarGridSpec(
            num_scalar_prefetch=1,
            grid=(1,),
            in_specs=[fixed(b.shape) for b in (*far, *accs)] + [rows, rows, columns],
            out_specs=[whole(wide.shape)] * 2 + [whole(part.shape)] * 2,
            scratch_shapes=[pltpu.VMEM((slots, pair), BF16)],
        ),
        out_shape=[wide, wide, part, part],
        compiler_params=params(32),
        cost_estimate=cost(10 * slots * width * quarter, 6 * quarter * width),
    )(order, *far, *accs, gate_mat, up_mat, down_mat)


def forward_hidden_kernel(groups, order_ref, rows_hbm, gate_hbm, up_hbm, down_hbm, *refs):
    hidden_ref, top_out, bottom_out, rows, gates, ups, down, gate_acc, up_acc, sems = refs
    quarter = rows.shape[2]
    far = pl.multiple_of(order_ref[groups - 1] * quarter, 128)
    copies = []
    for i in range(groups):
        block = pl.ds(i * quarter, quarter)
        copies.append(
            [
                pltpu.make_async_copy(rows_hbm.at[:, block], rows.at[i], sems.at[0, i]),
                pltpu.make_async_copy(gate_hbm.at[block], gates.at[i], sems.at[1, i]),
                pltpu.make_async_copy(up_hbm.at[block], ups.at[i], sems.at[2, i]),
            ]
        )
    last = pltpu.make_async_copy(down_hbm.at[:, pl.ds(far, quarter)], down, sems.at[3, 0])
    for group in copies:
        for copy in group:
            copy.start()
    last.start()
    for i, group in enumerate(copies):
        for copy in group:
            copy.wait()
        accumulate(i, gate_acc, dot(rows[i], gates[i]))
        accumulate(i, up_acc, dot(rows[i], ups[i]))
    gate_pre = gate_acc[...]
    hidden = (gate_pre * jax.nn.sigmoid(gate_pre) * up_acc[...]).astype(BF16)
    hidden_ref[...] = hidden
    last.wait()
    split(dot(hidden, down[...]), top_out, bottom_out)


def forward_hidden(order, rows, gate_mat, up_mat, down_mat, groups):
    slots, quarter = rows.shape[0], rows.shape[1] // groups
    width = gate_mat.shape[1]
    wide = jax.ShapeDtypeStruct((slots, width), BF16)
    part = jax.ShapeDtypeStruct((slots // 2, quarter), BF16)
    return pl.pallas_call(
        functools.partial(forward_hidden_kernel, groups),
        grid_spec=pltpu.PrefetchScalarGridSpec(
            num_scalar_prefetch=1,
            grid=(1,),
            in_specs=[pl.BlockSpec(memory_space=pl.ANY)] * 4,
            out_specs=[whole(wide.shape)] + [whole(part.shape)] * 2,
            scratch_shapes=[
                pltpu.VMEM((groups, slots, quarter), BF16),
                pltpu.VMEM((groups, quarter, width), BF16),
                pltpu.VMEM((groups, quarter, width), BF16),
                pltpu.VMEM((width, quarter), BF16),
                pltpu.VMEM((slots, width), F32),
                pltpu.VMEM((slots, width), F32),
                pltpu.SemaphoreType.DMA((4, groups)),
            ],
        ),
        out_shape=[wide, part, part],
        compiler_params=params(60),
        cost_estimate=cost(18 * slots * width * quarter, 18 * quarter * width),
    )(order, rows, gate_mat, up_mat, down_mat)


def forward_rest_kernel(order_ref, hidden_hbm, down_hbm, top_hbm, bottom_hbm, *refs):
    outs_hbm, (hidden, downs, far, outs, in_sems, out_sems) = refs[:2], refs[2:]
    quarter, half = outs.shape[2], far.shape[1]

    def block(i):
        start = pl.multiple_of(order_ref[i + 1] * quarter, 128)
        return down_hbm.at[:, pl.ds(start, quarter)]

    first = pltpu.make_async_copy(hidden_hbm, hidden, in_sems.at[0])
    weights = [pltpu.make_async_copy(block(i), downs.at[i], in_sems.at[1 + i]) for i in range(2)]
    sides = [
        pltpu.make_async_copy(ref, far.at[i], in_sems.at[3 + i])
        for i, ref in enumerate((top_hbm, bottom_hbm))
    ]
    sent = [
        pltpu.make_async_copy(outs.at[i], ref, out_sems.at[i]) for i, ref in enumerate(outs_hbm)
    ]
    first.start()
    weights[0].start()
    sides[0].start()
    weights[1].start()
    sides[1].start()
    first.wait()
    for i in range(2):
        weights[i].wait()
        part = dot(hidden[...], downs[i])
        sides[i].wait()
        if i == 0:
            outs[0, :half] = (part[:half] + far[0].astype(F32)).astype(BF16)
            outs[0, half:] = part[half:].astype(BF16)
        else:
            outs[1, :half] = part[:half].astype(BF16)
            outs[1, half:] = (part[half:] + far[1].astype(F32)).astype(BF16)
        sent[i].start()
    for copy in sent:
        copy.wait()


def forward_rest(order, hidden, down_mat, relayed, hint):
    slots, width = hidden.shape
    half, quarter = relayed[0].shape
    place = pl.BlockSpec(memory_space=pl.ANY)
    return pl.pallas_call(
        forward_rest_kernel,
        grid_spec=pltpu.PrefetchScalarGridSpec(
            num_scalar_prefetch=1,
            grid=(1,),
            in_specs=[place] * 4,
            out_specs=[place] * 2,
            scratch_shapes=[
                pltpu.VMEM((slots, width), BF16),
                pltpu.VMEM((2, width, quarter), BF16),
                pltpu.VMEM((2, half, quarter), BF16),
                pltpu.VMEM((2, slots, quarter), BF16),
                pltpu.SemaphoreType.DMA((5,)),
                pltpu.SemaphoreType.DMA((2,)),
            ],
        ),
        out_shape=[jax.ShapeDtypeStruct((slots, quarter), BF16)] * 2,
        compiler_params=params(60),
        cost_estimate=lasting(hint),
    )(order, hidden, down_mat, *relayed)


def forward_own_kernel(order_ref, hidden_ref, down_ref, out_ref):
    out_ref[...] = dot(hidden_ref[...], down_ref[...]).astype(BF16)


def forward_own(order, hidden, down_mat, quarter):
    slots, width = hidden.shape
    return pl.pallas_call(
        forward_own_kernel,
        grid_spec=pltpu.PrefetchScalarGridSpec(
            num_scalar_prefetch=1,
            grid=(1,),
            in_specs=[
                whole((slots, width)),
                pl.BlockSpec((width, quarter), lambda i, order: (0, order[0])),
            ],
            out_specs=whole((slots, quarter)),
        ),
        out_shape=jax.ShapeDtypeStruct((slots, quarter), BF16),
        compiler_params=params(32),
        cost_estimate=cost(2 * slots * width * quarter, 2 * quarter * (width + slots)),
    )(order, hidden, down_mat)


def backward_rest_kernel(order_ref, d_gate_ref, d_up_ref, gate_ref, up_ref, *out_refs):
    step = pl.program_id(0)
    part = dot_nt(d_gate_ref[...], gate_ref[...]) + dot_nt(d_up_ref[...], up_ref[...])
    part = part.astype(BF16)
    for number, out_ref in enumerate(out_refs):

        @pl.when(step == number)
        def _():
            out_ref[...] = part


def backward_rest(order, d_gate, d_up, gate_mat, up_mat, quarter):
    slots, width = d_gate.shape
    weight = pl.BlockSpec((quarter, width), lambda i, order: (order[(i + 1) % 3], 0))
    return pl.pallas_call(
        backward_rest_kernel,
        grid_spec=pltpu.PrefetchScalarGridSpec(
            num_scalar_prefetch=1,
            grid=(3,),
            in_specs=[whole((slots, width)), whole((slots, width)), weight, weight],
            out_specs=[whole((slots, quarter))] * 3,
        ),
        out_shape=[jax.ShapeDtypeStruct((slots, quarter), BF16)] * 3,
        compiler_params=params(32),
        cost_estimate=cost(12 * slots * width * quarter, 6 * quarter * (2 * width + slots)),
    )(order, d_gate, d_up, gate_mat, up_mat)


def relay_add_kernel(left_ref, right_ref, top_ref, bottom_ref, left_out, right_out):
    half = top_ref.shape[0]
    left_out[:half] = (left_ref[:half].astype(F32) + top_ref[...].astype(F32)).astype(BF16)
    left_out[half:] = left_ref[half:]
    right_out[:half] = right_ref[:half]
    right_out[half:] = (right_ref[half:].astype(F32) + bottom_ref[...].astype(F32)).astype(BF16)


def relay_add(left, right, top, bottom):
    shape = jax.ShapeDtypeStruct(left.shape, BF16)
    return pl.pallas_call(
        relay_add_kernel,
        out_shape=[shape, shape],
        compiler_params=params(24),
        cost_estimate=lasting(1),
    )(left, right, top, bottom)


def sum_kernel(a_ref, b_ref, c_ref, *refs):
    total = a_ref[...].astype(F32) + b_ref[...].astype(F32) + c_ref[...].astype(F32)
    refs[-1][...] = total.astype(BF16)


def summed(a, b, c, hint, after=()):
    return pl.pallas_call(
        sum_kernel,
        grid=(1,),
        in_specs=[whole(a.shape)] * 3 + [pl.BlockSpec(memory_space=pl.ANY)] * len(after),
        out_specs=whole(a.shape),
        out_shape=jax.ShapeDtypeStruct(a.shape, BF16),
        compiler_params=params(24),
        cost_estimate=lasting(hint),
    )(a, b, c, *after)


def exchange(rows, experts):
    slots, width = rows.shape
    blocks = rows.reshape(experts, slots // experts, width)
    return lax.all_to_all(blocks, "expert", split_axis=0, concat_axis=0, tiled=True).reshape(
        slots, width
    )


def local(x_fwd, ids_fwd, gates_fwd, x_bwd, ids_bwd, gates_bwd, grad_in, w_gate, w_up, w_down):
    experts = lax.axis_size("expert")
    groups = lax.axis_size("dp")
    dp_rank = lax.axis_index("dp")
    rows_dev = x_fwd.shape[1]
    topk = ids_fwd.shape[2]
    capacity = rows_dev * topk * 3 // (2 * experts)
    quarter = x_fwd.shape[2] // groups
    order = (dp_rank + jnp.array([0, groups - 1, 1, 2], jnp.int32)) % groups
    gate_mat = w_gate[0, 0]
    up_mat = w_up[0, 0]
    down_mat = w_down[0, 0]
    fwd_ids, fwd_gates = ids_fwd[0].T, gates_fwd[0].T
    bwd_ids, bwd_gates = ids_bwd[0].T, gates_bwd[0].T

    bwd_rows = pack_pair(bwd_ids, bwd_gates, grad_in[0], x_bwd[0], experts, capacity)
    bwd_rows = exchange(bwd_rows, experts)
    fwd_rows = pack(fwd_ids, x_fwd[0], experts, capacity)
    (bwd_rows,) = held((bwd_rows,), (fwd_rows,))
    fwd_rows = exchange(fwd_rows, experts)

    left, right = shifted(bwd_rows, "dp", 1), shifted(bwd_rows, "dp", -1)
    top, bottom = halves(left, right)
    far = shifted(top, "dp", 1), shifted(bottom, "dp", -1)
    accs = backward_early(order, (bwd_rows, left, right), gate_mat, up_mat, down_mat)
    d_gate, d_up, top, bottom = backward_late(order, far, accs, gate_mat, up_mat, down_mat)
    bwd_far = shifted(top, "dp", -1), shifted(bottom, "dp", 1)
    bwd_left, bwd_right, bwd_own = backward_rest(order, d_gate, d_up, gate_mat, up_mat, quarter)
    bwd_left, bwd_right = relay_add(bwd_left, bwd_right, *bwd_far)
    bwd_left, bwd_right = shifted(bwd_left, "dp", -1), shifted(bwd_right, "dp", 1)

    hidden, top, bottom = forward_hidden(order, fwd_rows, gate_mat, up_mat, down_mat, groups)
    fwd_far = shifted(top, "dp", -1), shifted(bottom, "dp", 1)
    bwd_back = exchange(summed(bwd_own, bwd_left, bwd_right, 20, (top,)), experts)

    fwd_left, fwd_right = forward_rest(order, hidden, down_mat, fwd_far, 40)
    fwd_own = forward_own(order, hidden, down_mat, quarter)
    fwd_left, fwd_right = shifted(fwd_left, "dp", -1), shifted(fwd_right, "dp", 1)
    fwd_back = exchange(summed(fwd_own, fwd_left, fwd_right, 1), experts)

    layer_grad = combine(bwd_ids, grad_in[0], bwd_back, experts, capacity)
    sent_backward = shifted(layer_grad[None], "pipe", -1)
    layer_out = combine_gated(order, fwd_ids, fwd_gates, x_fwd[0], fwd_back, experts, capacity)
    sent_forward = shifted(layer_out[None], "pipe", 1)
    return (sent_forward, sent_backward)


def solution(mesh):
    in_specs = (
        P("pipe", "expert", None),
        P("pipe", "expert", None),
        P("pipe", "expert", None),
        P("pipe", "expert", None),
        P("pipe", "expert", None),
        P("pipe", "expert", None),
        P("pipe", "expert", "dp"),
        P("pipe", "expert", None, "dp"),
        P("pipe", "expert", None, "dp"),
        P("pipe", "expert", "dp", None),
    )
    out_specs = (P("pipe", "expert", "dp"), P("pipe", "expert", "dp"))
    return jax.shard_map(local, mesh=mesh, in_specs=in_specs, out_specs=out_specs, check_vma=False)
```
